32 devices in a mesh: dp: 8 (over y, x, core), expert: 4 (over z).
Axes of the slice: x: 2, y: 2, z: 4, core: 2. Of those that a mesh axis runs over, the one named last changes fastest.
Arguments:
- grad: bfloat16 [4, 8, 256, 8192], P('expert', 'dp'), may hold values from -23 to 23, as said below
- error: bfloat16 [4, 8, 256, 8192], P('expert', 'dp'), may hold values from -3 to 3
- q_init: bfloat16 [4, 32, 8192], P('expert'), may hold values from -4 to 4
Outputs:
- basis_out: float32 [4, 256, 32], P('expert')
- q_factor: float32 [4, 32, 8192], P('expert', None, 'dp')
- new_error: bfloat16 [4, 8, 256, 8192], P('expert', 'dp')
- error_norm: float32 [], replicated
The draws below stay inside these ranges and needn't reach their ends.
Inputs may be any that keep to these rules, and one draw needn't show every extreme that they name: `grad`: entries of each expert's gradient.
All inputs are finite; a program needn't handle non-finite values.
Results may differ from the reference program's by a relative error of at most 0.02.
Values may be sent and summed in bfloat16 or wider, within the bound.
A program may use at most 64 MiB of HBM per device.

```python
import math
import jax
import jax.numpy as jnp
from jax import lax

ROWS = 256
FF = 8192
R = 32
ITERS = 2
EXPERTS = 4
REPLICAS = 8


def draw_grad(key, part):
    key = jax.random.fold_in(key, 7)
    key_base = jax.random.fold_in(key, 0)
    key_columns = jax.random.fold_in(key, 2)
    shape = (EXPERTS, REPLICAS, ROWS, FF)
    replica_ramp = jnp.arange(REPLICAS, dtype=jnp.float32) / max(REPLICAS - 1, 1)
    base = jax.random.truncated_normal(key_base, -4.0, 4.0, shape, jnp.float32)
    replica_scale = 0.5 * jnp.exp(replica_ramp * math.log(4.0))
    columns = jnp.exp(jax.random.uniform(key_columns, (EXPERTS, 1, 1, FF), jnp.float32, math.log(0.3), math.log(3.0)))
    ramp = jnp.arange(EXPERTS, dtype=jnp.float32) / max(EXPERTS - 1, 1)
    expert_scale = 0.6 * jnp.exp(ramp * math.log(3.0))
    values = base * columns * expert_scale[:, None, None, None] * replica_scale[None, :, None, None]
    return jnp.clip(values, -23.0, 23.0).astype(jnp.bfloat16)


def block_levels(rng, shape, shards, least, high):
    level, own = 1.0, jax.random.fold_in(rng, 6)
    for position, shards_of in shards:
        draws = jnp.exp(jax.random.uniform(jax.random.fold_in(own, position), (shards_of,), jnp.float32, least / len(shards), high / len(shards)))
        level = level * jnp.repeat(draws, shape[position] // shards_of).reshape([-1 if axis == position else 1 for axis in range(len(shape))])
    return level


def scatter_about(stream_key, dims, scale, most, cuts=(), held_as=jnp.bfloat16):
    gain = block_levels(stream_key, dims, cuts, -0.22, 0.18) if cuts else 1.0
    drawn = jax.random.normal(stream_key, dims, jnp.float32) * scale * gain
    return jnp.minimum(jnp.maximum(drawn, -most), most).astype(held_as)


def setup_inputs(seed: int = 0) -> dict:
    streams_of = jax.random.split(jax.random.key(seed), 4)
    return {
        "grad": draw_grad(jax.random.fold_in(streams_of[3], 71), 0),
        "error": scatter_about(streams_of[1], (EXPERTS, REPLICAS, ROWS, FF), 0.5, 3.0, ((0, 4), (1, 8))),
        "q_init": scatter_about(streams_of[2], (EXPERTS, R, FF), 1.0, 4.0, ((0, 4),)),
    }


def one_expert(pieces):
    grad_rows, error_rows, start_factor = pieces
    combined = (grad_rows.astype(jnp.float32) + error_rows.astype(jnp.float32)).astype(jnp.bfloat16)
    wide = combined.astype(jnp.float32)
    factor_low = start_factor
    orthonormal = jnp.zeros((ROWS, R), jnp.float32)
    ortho_low = orthonormal.astype(jnp.bfloat16)
    q_factor = jnp.zeros((R, FF), jnp.float32)
    for step in range(ITERS):
        projected = jnp.einsum('nrf,kf->rk', wide, factor_low.astype(jnp.float32), precision=lax.Precision.HIGHEST) / REPLICAS
        gram = jnp.dot(projected.T, projected, precision=lax.Precision.HIGHEST)
        lower_factor = jnp.linalg.cholesky(gram)
        orthonormal = jax.scipy.linalg.solve_triangular(lower_factor, projected.T, lower=True).T
        ortho_low = orthonormal.astype(jnp.bfloat16)
        q_factor = jnp.einsum('nrf,rk->kf', wide, ortho_low.astype(jnp.float32), precision=lax.Precision.HIGHEST) / REPLICAS
        factor_low = q_factor.astype(jnp.bfloat16)
    approx = jnp.dot(ortho_low.astype(jnp.float32), factor_low.astype(jnp.float32), preferred_element_type=jnp.float32)
    new_error = (wide - approx[None]).astype(jnp.bfloat16)
    squares = jnp.sum(jnp.square(new_error.astype(jnp.float32)))
    return (orthonormal, q_factor, new_error, squares)

def reference(grad, error, q_init):
    basis_out, q_factor, new_error, squares = lax.map(one_expert, (grad, error, q_init))
    count = EXPERTS * REPLICAS * ROWS * FF
    error_norm = jnp.sqrt(jnp.sum(squares) / count)
    return (basis_out, q_factor, new_error, error_norm)
```

```python
import functools

import jax
import jax.numpy as jnp
from jax import lax
from jax.experimental import pallas as pl
from jax.experimental.pallas import tpu as pltpu
from jax.sharding import PartitionSpec as P

ITERS = 2
MESH = pl.DeviceIdType.MESH
F32 = jnp.float32
BF16 = jnp.bfloat16
LANES = 128
GROUP = 8
NT = (((1,), (1,)), ((), ()))


def xor(a, b, size):
    out, bit = 0, 1
    while bit < size:
        out = out + bit * lax.rem(lax.div(a, bit) + lax.div(b, bit), 2)
        bit *= 2
    return out


def spread_row(tile, j):
    return jnp.broadcast_to(tile[j : j + 1, :], tile.shape)


def orthonormal_rows(pt):
    rank, rows = pt.shape
    groups, halves = rank // GROUP, rows // LANES
    padded = jnp.concatenate([pt, jnp.zeros((LANES - rank, rows), F32)], axis=0)
    gram = lax.dot_general(pt, padded, NT, precision=lax.Precision.HIGHEST, preferred_element_type=F32)
    g = [gram[GROUP * i : GROUP * (i + 1), :] for i in range(groups)]
    x = [
        [pt[GROUP * i : GROUP * (i + 1), LANES * h : LANES * (h + 1)] for h in range(halves)]
        for i in range(groups)
    ]
    row_id = lax.broadcasted_iota(jnp.int32, (GROUP, LANES), 0)
    for b in range(groups):
        below = range(b, groups)
        col = [
            {i: jnp.broadcast_to(g[i][:, GROUP * b + j : GROUP * b + j + 1], (GROUP, LANES)) for i in below}
            for j in range(GROUP)
        ]
        pivots = jnp.ones((GROUP, LANES), F32)
        for j in range(GROUP):
            pivot = spread_row(col[j][b], j)
            pivots = jnp.where(row_id == j, pivot, pivots)
            inverse = 1.0 / pivot
            factor = {i: col[j][i] * inverse for i in below}
            factor[b] = jnp.where(row_id > j, factor[b], 0.0)
            for k in range(j + 1, GROUP):
                row = spread_row(col[k][b], j)
                for i in below:
                    col[k][i] = col[k][i] - factor[i] * row
            for h in range(halves):
                row = spread_row(x[b][h], j)
                for i in below:
                    x[i][h] = x[i][h] - factor[i] * row
            if b + 1 < groups:
                row = spread_row(g[b], j)
                for i in below:
                    g[i] = g[i] - factor[i] * row
        scale = lax.rsqrt(pivots)
        for h in range(halves):
            x[b][h] = x[b][h] * scale
    return jnp.concatenate([jnp.concatenate(parts, axis=1) for parts in x], axis=0)


def kernel(
    n, experts, count,
    grad, error, q_init,
    basis, q_out, new_error, norm,
    g_buf, e_buf, comb, fac0, fac, keep,
    s1_send, s1_recv, s2_send, s2_recv, p1, p1_recv, p2, n1, n2,
    g_sem, e_sem, q_sem, o_sem,
    s1_ss, s1_rs, s2_ss, s2_rs, p1_ss, p1_rs, p2_ss, p2_rs,
    ag_ss, fw_ss, ag_rs, n1_ss, n1_rs, n2_ss, n2_rs,
):
    me = lax.axis_index("dp")
    place = lax.axis_index("expert")
    chip, core = lax.div(me, 2), lax.rem(me, 2)
    partner = 2 * chip + 1 - core
    chips = n // 2
    rows, share = comb.shape[1], comb.shape[2]

    def send(src, dst, ssem, rsem, **where):
        return pltpu.make_async_remote_copy(
            src_ref=src, dst_ref=dst, send_sem=ssem, recv_sem=rsem, device_id=where, device_id_type=MESH
        )

    def columns(ref, j):
        return ref.at[:, pl.ds(pl.multiple_of(j * share, share), share)]

    def load(j):
        return (
            pltpu.make_async_copy(columns(grad, j), g_buf.at[j], g_sem.at[j]),
            pltpu.make_async_copy(columns(error, j), e_buf.at[j], e_sem.at[j]),
            pltpu.make_async_copy(columns(q_init, j), fac0.at[j], q_sem.at[j]),
        )

    for j in range(n):
        for copy in load(j):
            copy.start()

    barrier = pltpu.get_barrier_semaphore()
    for s in range(1, n):
        pl.semaphore_signal(barrier, inc=1, device_id={"dp": lax.rem(me + s, n)}, device_id_type=MESH)
    for s in range(1, experts):
        pl.semaphore_signal(
            barrier, inc=1, device_id={"expert": lax.rem(place + s, experts)}, device_id_type=MESH
        )

    def first(j, total):
        for copy in load(j):
            copy.wait()
        comb[j] = (g_buf[j].astype(F32) + e_buf[j].astype(F32)).astype(BF16)
        return total + lax.dot_general(fac0[j], comb[j], NT, preferred_element_type=F32)

    total = lax.fori_loop(0, n, first, jnp.zeros(p1.shape[1:], F32))
    pl.semaphore_wait(barrier, n - 1 + experts - 1)

    pending = []
    for it in range(ITERS):
        last = it == ITERS - 1
        p1[it] = total
        copy = send(p1.at[it], p1_recv.at[it], p1_ss.at[it], p1_rs.at[it], dp=partner)
        copy.start()
        pending.append(copy)
        copy.wait_recv()
        p2[it, chip] = p1[it] + p1_recv[it]
        copies = []
        for s in range(chips - 1, 0, -1):
            copies.append(
                send(
                    p2.at[it, chip], p2.at[it, chip], p2_ss.at[it, s], p2_rs.at[it, s],
                    dp=2 * xor(chip, s, chips) + core,
                )
            )
            copies[-1].start()
        for copy in copies:
            copy.wait_recv()
        pending += copies
        pt = p2[it, 0]
        for t in range(1, chips):
            pt = pt + p2[it, t]
        pt = pt / n
        ortho = orthonormal_rows(pt)
        low = ortho.astype(BF16)

        def finish(s):
            copy = first_hop[s]
            copy.wait_recv()
            both = keep[s] + s1_recv[it, s].astype(F32)
            if s == 0:
                return both
            s2_send[it, s] = both.astype(BF16)
            copy = send(
                s2_send.at[it, s], s2_recv.at[it, s], s2_ss.at[it, s], s2_rs.at[it, s],
                dp=2 * xor(chip, s, chips) + core,
            )
            copy.start()
            second_hop.append(copy)
            return None

        first_hop, second_hop = {}, []
        for s in range(chips - 1, -1, -1):
            t = xor(chip, s, chips)
            s1_send[it, s] = jnp.dot(
                low, comb[2 * t + 1 - core], preferred_element_type=F32
            ).astype(BF16)
            first_hop[s] = send(
                s1_send.at[it, s], s1_recv.at[it, s], s1_ss.at[it, s], s1_rs.at[it, s], dp=partner
            )
            first_hop[s].start()
            keep[s] = jnp.dot(low, comb[2 * t + core], preferred_element_type=F32)
            if s + 1 < chips:
                finish(s + 1)
        q = finish(0)
        if last:
            ortho_t = jnp.transpose(ortho)
            basis[...] = ortho_t
            low_t = ortho_t.astype(BF16)
        for copy in second_hop:
            copy.wait_recv()
        for s in range(1, chips):
            q = q + s2_recv[it, s].astype(F32)
        q = q / n
        pending += list(first_hop.values()) + second_hop
        if last:
            q_out[...] = q
        fac[it, me] = q.astype(BF16)

        for s in range(chips - 1, -1, -1):
            target = partner if s == 0 else 2 * xor(chip, s, chips) + core
            copy = send(fac.at[it, me], fac.at[it, me], ag_ss.at[it, s], ag_rs.at[it, me], dp=target)
            copy.start()
            pending.append(copy)

        def block(j, it=it):
            return fac.at[it, j]

        def arrived(j, it=it):
            send(fac.at[it, j], fac.at[it, j], fw_ss.at[it, 0], ag_rs.at[it, j], dp=partner).wait_recv()

        def forward(s, j, it=it):
            return send(fac.at[it, j], fac.at[it, j], fw_ss.at[it, s], ag_rs.at[it, j], dp=partner)

        if not last:
            def use(j, value, it=it):
                return value + lax.dot_general(fac[it, j], comb[j], NT, preferred_element_type=F32)

            value = jnp.zeros(p1.shape[1:], F32)
        else:
            def use(j, value, it=it):
                approx = jnp.dot(low_t, fac[it, j], preferred_element_type=F32)
                residual = (comb[j].astype(F32) - approx).astype(BF16)
                g_buf[j] = residual
                pltpu.make_async_copy(g_buf.at[j], columns(new_error, j), o_sem.at[j]).start()
                wide = residual.astype(F32)
                squares = jnp.sum((wide * wide).reshape(rows // GROUP, GROUP, share), axis=0)
                for h in range(share // LANES):
                    value = value + squares[:, LANES * h : LANES * (h + 1)]
                return value

            value = jnp.zeros(n1.shape[1:], F32)

        value = use(me, value)
        arrived(partner)
        value = use(partner, value)

        def step(s, value, use=use):
            t = xor(chip, s, chips)
            arrived(2 * t + core)
            forward(s, 2 * t + core).start()
            value = use(2 * t + core, value)
            arrived(2 * t + 1 - core)
            return use(2 * t + 1 - core, value)

        total = lax.fori_loop(1, chips, step, value)

    n1[me] = total
    copies = [
        send(n1.at[me], n1.at[me], n1_ss.at[s], n1_rs.at[s], dp=lax.rem(me + s, n)) for s in range(1, n)
    ]
    for copy in copies:
        copy.start()
    for copy in copies:
        copy.wait_recv()
    pending += copies
    total = n1[0]
    for j in range(1, n):
        total = total + n1[j]
    n2[place] = total
    copies = [
        send(n2.at[place], n2.at[place], n2_ss.at[s], n2_rs.at[s], expert=lax.rem(place + s, experts))
        for s in range(1, experts)
    ]
    for copy in copies:
        copy.start()
    for copy in copies:
        copy.wait_recv()
    pending += copies
    total = n2[0]
    for j in range(1, experts):
        total = total + n2[j]
    norm[...] = jnp.sqrt(jnp.sum(total, keepdims=True) / count)

    for copy in pending:
        copy.wait_send()
    for it in range(ITERS):
        for s in range(1, chips):
            j = 2 * xor(chip, s, chips) + core
            send(fac.at[it, j], fac.at[it, j], fw_ss.at[it, s], ag_rs.at[it, j], dp=partner).wait_send()
    for j in range(n):
        pltpu.make_async_copy(g_buf.at[j], columns(new_error, j), o_sem.at[j]).wait()


def local(grad, error, q_init):
    n, experts = lax.axis_size("dp"), lax.axis_size("expert")
    rows, width = grad.shape[2:]
    rank = q_init.shape[1]
    share = width // n
    chips = n // 2
    count = rows * width * n * experts
    dma = pltpu.SemaphoreType.DMA
    vmem, hbm = pl.BlockSpec(memory_space=pltpu.VMEM), pl.BlockSpec(memory_space=pl.ANY)
    hop = pltpu.VMEM((ITERS, chips, rank, share), BF16)
    basis, q, new_error, norm = pl.pallas_call(
        functools.partial(kernel, n, experts, count),
        out_shape=(
            jax.ShapeDtypeStruct((rows, rank), F32),
            jax.ShapeDtypeStruct((rank, share), F32),
            jax.ShapeDtypeStruct((rows, width), BF16),
            jax.ShapeDtypeStruct((1, 1), F32),
        ),
        in_specs=[hbm, hbm, hbm],
        out_specs=(vmem, vmem, hbm, vmem),
        scratch_shapes=[
            pltpu.VMEM((n, rows, share), BF16),
            pltpu.VMEM((n, rows, share), BF16),
            pltpu.VMEM((n, rows, share), BF16),
            pltpu.VMEM((n, rank, share), BF16),
            pltpu.VMEM((ITERS, n, rank, share), BF16),
            pltpu.VMEM((chips, rank, share), F32),
            hop, hop, hop, hop,
            pltpu.VMEM((ITERS, rank, rows), F32),
            pltpu.VMEM((ITERS, rank, rows), F32),
            pltpu.VMEM((ITERS, chips, rank, rows), F32),
            pltpu.VMEM((n, GROUP, LANES), F32),
            pltpu.VMEM((experts, GROUP, LANES), F32),
            dma((n,)), dma((n,)), dma((n,)), dma((n,)),
            dma((ITERS, chips)), dma((ITERS, chips)), dma((ITERS, chips)), dma((ITERS, chips)),
            dma((ITERS,)), dma((ITERS,)), dma((ITERS, chips)), dma((ITERS, chips)),
            dma((ITERS, chips)), dma((ITERS, chips)), dma((ITERS, n)),
            dma((n,)), dma((n,)), dma((experts,)), dma((experts,)),
        ],
        compiler_params=pltpu.CompilerParams(
            collective_id=0, has_side_effects=True, vmem_limit_bytes=56 * 2**20
        ),
        cost_estimate=pl.CostEstimate(
            flops=2 * 5 * rows * rank * width, bytes_accessed=6 * rows * width, transcendentals=0
        ),
    )(grad[0, 0], error[0, 0], q_init[0])
    return (basis[None], q[None], new_error[None, None], norm[0, 0])


def solution(mesh):
    placed = (P("expert", "dp", None, None), P("expert", "dp", None, None), P("expert", None, None))
    return jax.shard_map(
        local,
        mesh=mesh,
        in_specs=placed,
        out_specs=(
            P("expert", None, None),
            P("expert", None, "dp"),
            P("expert", "dp", None, None),
            P(),
        ),
        check_vma=False,
    )
```

```python
import functools

import jax
import jax.numpy as jnp
from jax import lax
from jax.experimental import pallas as pl
from jax.experimental.pallas import tpu as pltpu
from jax.sharding import PartitionSpec as P

ITERS = 2
MESH = pl.DeviceIdType.MESH
F32 = jnp.float32
BF16 = jnp.bfloat16
LANES = 128
GROUP = 8
NT = (((1,), (1,)), ((), ()))


def xor(a, b, size):
    out, bit = 0, 1
    while bit < size:
        out = out + bit * lax.rem(lax.div(a, bit) + lax.div(b, bit), 2)
        bit *= 2
    return out


def spread_row(tile, j):
    return jnp.broadcast_to(tile[j : j + 1, :], tile.shape)


def orthonormal_rows(pt):
    rank, rows = pt.shape
    groups, halves = rank // GROUP, rows // LANES
    padded = jnp.concatenate([pt, jnp.zeros((LANES - rank, rows), F32)], axis=0)
    gram = lax.dot_general(pt, padded, NT, precision=lax.Precision.HIGHEST, preferred_element_type=F32)
    g = [gram[GROUP * i : GROUP * (i + 1), :] for i in range(groups)]
    x = [
        [pt[GROUP * i : GROUP * (i + 1), LANES * h : LANES * (h + 1)] for h in range(halves)]
        for i in range(groups)
    ]
    row_id = lax.broadcasted_iota(jnp.int32, (GROUP, LANES), 0)
    for b in range(groups):
        below = range(b, groups)
        col = [
            {i: jnp.broadcast_to(g[i][:, GROUP * b + j : GROUP * b + j + 1], (GROUP, LANES)) for i in below}
            for j in range(GROUP)
        ]
        pivots = jnp.ones((GROUP, LANES), F32)
        for j in range(GROUP):
            pivot = spread_row(col[j][b], j)
            pivots = jnp.where(row_id == j, pivot, pivots)
            inverse = 1.0 / pivot
            factor = {i: col[j][i] * inverse for i in below}
            factor[b] = jnp.where(row_id > j, factor[b], 0.0)
            for k in range(j + 1, GROUP):
                row = spread_row(col[k][b], j)
                for i in below:
                    col[k][i] = col[k][i] - factor[i] * row
            for h in range(halves):
                row = spread_row(x[b][h], j)
                for i in below:
                    x[i][h] = x[i][h] - factor[i] * row
            if b + 1 < groups:
                row = spread_row(g[b], j)
                for i in below:
                    g[i] = g[i] - factor[i] * row
        scale = lax.rsqrt(pivots)
        for h in range(halves):
            x[b][h] = x[b][h] * scale
    return jnp.concatenate([jnp.concatenate(parts, axis=1) for parts in x], axis=0)


def kernel(
    n, experts, count,
    grad, error, q_init,
    basis, q_out, new_error, norm,
    g_buf, e_buf, comb, fac0, fac, keep,
    s1_send, s1_recv, s2_send, s2_recv, p1, p1_recv, p2, n1, n2,
    g_sem, e_sem, q_sem, o_sem,
    s1_ss, s1_rs, s2_ss, s2_rs, p1_ss, p1_rs, p2_ss, p2_rs,
    ag_ss, fw_ss, ag_rs, n1_ss, n1_rs, n2_ss, n2_rs,
):
    me = lax.axis_index("dp")
    place = lax.axis_index("expert")
    chip, core = lax.div(me, 2), lax.rem(me, 2)
    partner = 2 * chip + 1 - core
    chips = n // 2
    rows, share, rank = comb.shape[1], comb.shape[2], fac0.shape[1]

    def send(src, dst, ssem, rsem, **where):
        return pltpu.make_async_remote_copy(
            src_ref=src, dst_ref=dst, send_sem=ssem, recv_sem=rsem, device_id=where, device_id_type=MESH
        )

    def columns(ref, j):
        return ref.at[:, pl.ds(pl.multiple_of(j * share, share), share)]

    def load(j):
        return (
            pltpu.make_async_copy(columns(grad, j), g_buf.at[j], g_sem.at[j]),
            pltpu.make_async_copy(columns(error, j), e_buf.at[j], e_sem.at[j]),
            pltpu.make_async_copy(columns(q_init, j), fac0.at[j], q_sem.at[j]),
        )

    for j in range(n):
        for copy in load(j):
            copy.start()

    barrier = pltpu.get_barrier_semaphore()
    for s in range(1, n):
        pl.semaphore_signal(barrier, inc=1, device_id={"dp": lax.rem(me + s, n)}, device_id_type=MESH)
    for s in range(1, experts):
        pl.semaphore_signal(
            barrier, inc=1, device_id={"expert": lax.rem(place + s, experts)}, device_id_type=MESH
        )

    def first(j, total):
        for copy in load(j):
            copy.wait()
        comb[j] = (g_buf[j].astype(F32) + e_buf[j].astype(F32)).astype(BF16)
        return total + lax.dot_general(comb[j], fac0[j], NT, preferred_element_type=F32)

    total = lax.fori_loop(0, n, first, jnp.zeros((rows, rank), F32))
    pl.semaphore_wait(barrier, n - 1 + experts - 1)

    pending = []
    for it in range(ITERS):
        last = it == ITERS - 1
        p1[it] = jnp.transpose(total)
        copy = send(p1.at[it], p1_recv.at[it], p1_ss.at[it], p1_rs.at[it], dp=partner)
        copy.start()
        pending.append(copy)
        copy.wait_recv()
        p2[it, chip] = p1[it] + p1_recv[it]
        copies = []
        for s in range(chips - 1, 0, -1):
            copies.append(
                send(
                    p2.at[it, chip], p2.at[it, chip], p2_ss.at[it, s], p2_rs.at[it, s],
                    dp=2 * xor(chip, s, chips) + core,
                )
            )
            copies[-1].start()
        for copy in copies:
            copy.wait_recv()
        pending += copies
        pt = p2[it, 0]
        for t in range(1, chips):
            pt = pt + p2[it, t]
        pt = pt / n
        ortho = orthonormal_rows(pt)
        low = ortho.astype(BF16)

        def finish(s):
            copy = first_hop[s]
            copy.wait_recv()
            both = keep[s] + s1_recv[it, s].astype(F32)
            if s == 0:
                return both
            s2_send[it, s] = both.astype(BF16)
            copy = send(
                s2_send.at[it, s], s2_recv.at[it, s], s2_ss.at[it, s], s2_rs.at[it, s],
                dp=2 * xor(chip, s, chips) + core,
            )
            copy.start()
            second_hop.append(copy)
            return None

        first_hop, second_hop = {}, []
        for s in range(chips - 1, -1, -1):
            t = xor(chip, s, chips)
            s1_send[it, s] = jnp.dot(
                low, comb[2 * t + 1 - core], preferred_element_type=F32
            ).astype(BF16)
            first_hop[s] = send(
                s1_send.at[it, s], s1_recv.at[it, s], s1_ss.at[it, s], s1_rs.at[it, s], dp=partner
            )
            first_hop[s].start()
            keep[s] = jnp.dot(low, comb[2 * t + core], preferred_element_type=F32)
            if s + 1 < chips:
                finish(s + 1)
        q = finish(0)
        if last:
            basis[...] = ortho
            low_t = jnp.transpose(ortho).astype(BF16)
        for copy in second_hop:
            copy.wait_recv()
        for s in range(1, chips):
            q = q + s2_recv[it, s].astype(F32)
        q = q / n
        pending += list(first_hop.values()) + second_hop
        if last:
            q_out[...] = q
        fac[it, me] = q.astype(BF16)

        for s in range(chips - 1, -1, -1):
            target = partner if s == 0 else 2 * xor(chip, s, chips) + core
            copy = send(fac.at[it, me], fac.at[it, me], ag_ss.at[it, s], ag_rs.at[it, me], dp=target)
            copy.start()
            pending.append(copy)

        def block(j, it=it):
            return fac.at[it, j]

        def arrived(j, it=it):
            send(fac.at[it, j], fac.at[it, j], fw_ss.at[it, 0], ag_rs.at[it, j], dp=partner).wait_recv()

        def forward(s, j, it=it):
            return send(fac.at[it, j], fac.at[it, j], fw_ss.at[it, s], ag_rs.at[it, j], dp=partner)

        if not last:
            def use(j, value, it=it):
                return value + lax.dot_general(comb[j], fac[it, j], NT, preferred_element_type=F32)

            value = jnp.zeros((rows, rank), F32)
        else:
            def use(j, value, it=it):
                approx = jnp.dot(low_t, fac[it, j], preferred_element_type=F32)
                residual = (comb[j].astype(F32) - approx).astype(BF16)
                g_buf[j] = residual
                pltpu.make_async_copy(g_buf.at[j], columns(new_error, j), o_sem.at[j]).start()
                wide = residual.astype(F32)
                squares = jnp.sum((wide * wide).reshape(rows // GROUP, GROUP, share), axis=0)
                for h in range(share // LANES):
                    value = value + squares[:, LANES * h : LANES * (h + 1)]
                return value

            value = jnp.zeros(n1.shape[1:], F32)

        value = use(me, value)
        arrived(partner)
        value = use(partner, value)

        def step(s, value, use=use):
            t = xor(chip, s, chips)
            arrived(2 * t + core)
            forward(s, 2 * t + core).start()
            value = use(2 * t + core, value)
            arrived(2 * t + 1 - core)
            return use(2 * t + 1 - core, value)

        total = lax.fori_loop(1, chips, step, value)

    n1[me] = total
    copies = [
        send(n1.at[me], n1.at[me], n1_ss.at[s], n1_rs.at[s], dp=lax.rem(me + s, n)) for s in range(1, n)
    ]
    for copy in copies:
        copy.start()
    for copy in copies:
        copy.wait_recv()
    pending += copies
    total = n1[0]
    for j in range(1, n):
        total = total + n1[j]
    n2[place] = total
    copies = [
        send(n2.at[place], n2.at[place], n2_ss.at[s], n2_rs.at[s], expert=lax.rem(place + s, experts))
        for s in range(1, experts)
    ]
    for copy in copies:
        copy.start()
    for copy in copies:
        copy.wait_recv()
    pending += copies
    total = n2[0]
    for j in range(1, experts):
        total = total + n2[j]
    norm[...] = jnp.sqrt(jnp.sum(total, keepdims=True) / count)

    for copy in pending:
        copy.wait_send()
    for it in range(ITERS):
        for s in range(1, chips):
            j = 2 * xor(chip, s, chips) + core
            send(fac.at[it, j], fac.at[it, j], fw_ss.at[it, s], ag_rs.at[it, j], dp=partner).wait_send()
    for j in range(n):
        pltpu.make_async_copy(g_buf.at[j], columns(new_error, j), o_sem.at[j]).wait()


def hand_out_kernel(basis, q, new_error, basis_out, q_out, new_error_out, sems):
    parts = sems.shape[0] - 2
    height = new_error.shape[0] // parts
    copies = [
        pltpu.make_async_copy(
            new_error.at[pl.ds(i * height, height), :], new_error_out.at[pl.ds(i * height, height), :], sems.at[i]
        )
        for i in range(parts)
    ]
    copies.append(pltpu.make_async_copy(basis, basis_out, sems.at[parts]))
    copies.append(pltpu.make_async_copy(q, q_out, sems.at[parts + 1]))
    for copy in copies:
        copy.start()
    for copy in copies:
        copy.wait()


def hand_out(*arrays):
    hbm = pl.BlockSpec(memory_space=pl.ANY)
    return pl.pallas_call(
        hand_out_kernel,
        out_shape=tuple(jax.ShapeDtypeStruct(a.shape, a.dtype) for a in arrays),
        in_specs=[hbm] * 3,
        out_specs=(hbm,) * 3,
        scratch_shapes=[pltpu.SemaphoreType.DMA((16 + 2,))],
        compiler_params=pltpu.CompilerParams(vmem_limit_bytes=60 * 2**20),
    )(*arrays)


def local(grad, error, q_init):
    n, experts = lax.axis_size("dp"), lax.axis_size("expert")
    rows, width = grad.shape[2:]
    rank = q_init.shape[1]
    share = width // n
    chips = n // 2
    count = rows * width * n * experts
    dma = pltpu.SemaphoreType.DMA
    vmem, hbm = pl.BlockSpec(memory_space=pltpu.VMEM), pl.BlockSpec(memory_space=pl.ANY)
    hop = pltpu.VMEM((ITERS, chips, rank, share), BF16)
    basis, q, new_error, norm = pl.pallas_call(
        functools.partial(kernel, n, experts, count),
        out_shape=(
            jax.ShapeDtypeStruct((rank, rows), F32),
            jax.ShapeDtypeStruct((rank, share), F32),
            jax.ShapeDtypeStruct((rows, width), BF16),
            jax.ShapeDtypeStruct((1, 1), F32),
        ),
        in_specs=[hbm, hbm, hbm],
        out_specs=(vmem, vmem, hbm, vmem),
        scratch_shapes=[
            pltpu.VMEM((n, rows, share), BF16),
            pltpu.VMEM((n, rows, share), BF16),
            pltpu.VMEM((n, rows, share), BF16),
            pltpu.VMEM((n, rank, share), BF16),
            pltpu.VMEM((ITERS, n, rank, share), BF16),
            pltpu.VMEM((chips, rank, share), F32),
            hop, hop, hop, hop,
            pltpu.VMEM((ITERS, rank, rows), F32),
            pltpu.VMEM((ITERS, rank, rows), F32),
            pltpu.VMEM((ITERS, chips, rank, rows), F32),
            pltpu.VMEM((n, GROUP, LANES), F32),
            pltpu.VMEM((experts, GROUP, LANES), F32),
            dma((n,)), dma((n,)), dma((n,)), dma((n,)),
            dma((ITERS, chips)), dma((ITERS, chips)), dma((ITERS, chips)), dma((ITERS, chips)),
            dma((ITERS,)), dma((ITERS,)), dma((ITERS, chips)), dma((ITERS, chips)),
            dma((ITERS, chips)), dma((ITERS, chips)), dma((ITERS, n)),
            dma((n,)), dma((n,)), dma((experts,)), dma((experts,)),
        ],
        compiler_params=pltpu.CompilerParams(
            collective_id=0, has_side_effects=True, vmem_limit_bytes=56 * 2**20
        ),
        cost_estimate=pl.CostEstimate(
            flops=2 * 5 * rows * rank * width, bytes_accessed=6 * rows * width, transcendentals=0
        ),
    )(grad[0, 0], error[0, 0], q_init[0])
    basis, q, new_error = hand_out(basis, q, new_error)
    return (jnp.transpose(basis)[None], q[None], new_error[None, None], norm[0, 0])


def solution(mesh):
    placed = (P("expert", "dp", None, None), P("expert", "dp", None, None), P("expert", None, None))
    return jax.shard_map(
        local,
        mesh=mesh,
        in_specs=placed,
        out_specs=(
            P("expert", None, None),
            P("expert", None, "dp"),
            P("expert", "dp", None, None),
            P(),
        ),
        check_vma=False,
    )
```

```python
import functools

import jax
import jax.numpy as jnp
from jax import lax
from jax.experimental import pallas as pl
from jax.experimental.pallas import tpu as pltpu
from jax.sharding import PartitionSpec as P

ITERS = 2
MESH = pl.DeviceIdType.MESH
F32 = jnp.float32
BF16 = jnp.bfloat16
LANES = 128
GROUP = 8
NT = (((1,), (1,)), ((), ()))


def xor(a, b, size):
    out, bit = 0, 1
    while bit < size:
        out = out + bit * lax.rem(lax.div(a, bit) + lax.div(b, bit), 2)
        bit *= 2
    return out


def spread_row(tile, j):
    return jnp.broadcast_to(tile[j : j + 1, :], tile.shape)


def orthonormal_rows(pt):
    rank, rows = pt.shape
    groups, halves = rank // GROUP, rows // LANES
    padded = jnp.concatenate([pt, jnp.zeros((LANES - rank, rows), F32)], axis=0)
    gram = lax.dot_general(pt, padded, NT, precision=lax.Precision.HIGHEST, preferred_element_type=F32)
    g = [gram[GROUP * i : GROUP * (i + 1), :] for i in range(groups)]
    x = [
        [pt[GROUP * i : GROUP * (i + 1), LANES * h : LANES * (h + 1)] for h in range(halves)]
        for i in range(groups)
    ]
    row_id = lax.broadcasted_iota(jnp.int32, (GROUP, LANES), 0)
    for b in range(groups):
        below = range(b, groups)
        col = [
            {i: jnp.broadcast_to(g[i][:, GROUP * b + j : GROUP * b + j + 1], (GROUP, LANES)) for i in below}
            for j in range(GROUP)
        ]
        pivots = jnp.ones((GROUP, LANES), F32)
        for j in range(GROUP):
            pivot = spread_row(col[j][b], j)
            pivots = jnp.where(row_id == j, pivot, pivots)
            inverse = 1.0 / pivot
            factor = {i: col[j][i] * inverse for i in below}
            factor[b] = jnp.where(row_id > j, factor[b], 0.0)
            for k in range(j + 1, GROUP):
                row = spread_row(col[k][b], j)
                for i in below:
                    col[k][i] = col[k][i] - factor[i] * row
            for h in range(halves):
                row = spread_row(x[b][h], j)
                for i in below:
                    x[i][h] = x[i][h] - factor[i] * row
            if b + 1 < groups:
                row = spread_row(g[b], j)
                for i in below:
                    g[i] = g[i] - factor[i] * row
        scale = lax.rsqrt(pivots)
        for h in range(halves):
            x[b][h] = x[b][h] * scale
    return jnp.concatenate([jnp.concatenate(parts, axis=1) for parts in x], axis=0)


def kernel(
    n, experts, count,
    grad, error, q_init,
    basis, q_out, new_error, norm,
    g_buf, e_buf, comb, theirs, pair, fac0, fac,
    s2_send, s2_recv, p1, p1_recv, p2, n1, n2,
    g_sem, e_sem, q_sem, o_sem,
    s1_ss, s1_rs, s2_ss, s2_rs, p1_ss, p1_rs, p2_ss, p2_rs,
    ag_ss, fw_ss, ag_rs, n1_ss, n1_rs, n2_ss, n2_rs,
):
    me = lax.axis_index("dp")
    place = lax.axis_index("expert")
    chip, core = lax.div(me, 2), lax.rem(me, 2)
    partner = 2 * chip + 1 - core
    chips = n // 2
    rows, share, rank = comb.shape[1], comb.shape[2], fac0.shape[1]

    def send(src, dst, ssem, rsem, **where):
        return pltpu.make_async_remote_copy(
            src_ref=src, dst_ref=dst, send_sem=ssem, recv_sem=rsem, device_id=where, device_id_type=MESH
        )

    def columns(ref, j):
        return ref.at[:, pl.ds(pl.multiple_of(j * share, share), share)]

    def load(j):
        return (
            pltpu.make_async_copy(columns(grad, j), g_buf.at[j], g_sem.at[j]),
            pltpu.make_async_copy(columns(error, j), e_buf.at[j], e_sem.at[j]),
        )

    def load_factor(t):
        return pltpu.make_async_copy(columns(q_init, 2 * t + core), fac0.at[t], q_sem.at[t])

    def combine(j):
        for copy in load(j):
            copy.wait()
        comb[j] = (g_buf[j].astype(F32) + e_buf[j].astype(F32)).astype(BF16)

    def hand_over(t):
        return send(comb.at[2 * t + 1 - core], theirs.at[t], s1_ss.at[t], s1_rs.at[t], dp=partner)

    for t in range(chips):
        for copy in load(2 * t + 1 - core):
            copy.start()
    for t in range(chips):
        for copy in load(2 * t + core):
            copy.start()
        load_factor(t).start()

    barrier = pltpu.get_barrier_semaphore()
    for s in range(1, n):
        pl.semaphore_signal(barrier, inc=1, device_id={"dp": lax.rem(me + s, n)}, device_id_type=MESH)
    for s in range(1, experts):
        pl.semaphore_signal(
            barrier, inc=1, device_id={"expert": lax.rem(place + s, experts)}, device_id_type=MESH
        )

    combine(1 - core)
    pl.semaphore_wait(barrier, n - 1 + experts - 1)
    hand_over(0).start()

    def first(t, _):
        combine(2 * t + 1 - core)
        hand_over(t).start()
        return 0

    lax.fori_loop(1, chips, first, 0)

    def second(t, total):
        combine(2 * t + core)
        load_factor(t).wait()
        hand_over(t).wait_recv()
        pair[t] = (comb[2 * t + core].astype(F32) + theirs[t].astype(F32)).astype(BF16)
        return total + lax.dot_general(pair[t], fac0[t], NT, preferred_element_type=F32)

    total = lax.fori_loop(0, chips, second, jnp.zeros((rows, rank), F32))

    pending = []
    for it in range(ITERS):
        last = it == ITERS - 1
        p1[it] = jnp.transpose(total)
        copy = send(p1.at[it], p1_recv.at[it], p1_ss.at[it], p1_rs.at[it], dp=partner)
        copy.start()
        pending.append(copy)
        copy.wait_recv()
        p2[it, chip] = p1[it] + p1_recv[it]
        copies = []
        for s in range(chips - 1, 0, -1):
            copies.append(
                send(
                    p2.at[it, chip], p2.at[it, chip], p2_ss.at[it, s], p2_rs.at[it, s],
                    dp=2 * xor(chip, s, chips) + core,
                )
            )
            copies[-1].start()
        for copy in copies:
            copy.wait_recv()
        pending += copies
        pt = p2[it, 0]
        for t in range(1, chips):
            pt = pt + p2[it, t]
        pt = pt / n
        ortho = orthonormal_rows(pt)
        low = ortho.astype(BF16)

        second_hop = []
        for s in range(chips - 1, -1, -1):
            q = jnp.dot(low, pair[xor(chip, s, chips)], preferred_element_type=F32)
            if s:
                s2_send[it, s] = q.astype(BF16)
                second_hop.append(
                    send(
                        s2_send.at[it, s], s2_recv.at[it, s], s2_ss.at[it, s], s2_rs.at[it, s],
                        dp=2 * xor(chip, s, chips) + core,
                    )
                )
                second_hop[-1].start()
        if last:
            basis[...] = ortho
            low_t = jnp.transpose(ortho).astype(BF16)
        for copy in second_hop:
            copy.wait_recv()
        for s in range(1, chips):
            q = q + s2_recv[it, s].astype(F32)
        q = q / n
        pending += second_hop
        if last:
            q_out[...] = q
        fac[it, me] = q.astype(BF16)

        for s in range(chips - 1, -1 if last else 0, -1):
            target = partner if s == 0 else 2 * xor(chip, s, chips) + core
            copy = send(fac.at[it, me], fac.at[it, me], ag_ss.at[it, s], ag_rs.at[it, me], dp=target)
            copy.start()
            pending.append(copy)

        def forward(s, j, it=it):
            return send(fac.at[it, j], fac.at[it, j], fw_ss.at[s], ag_rs.at[it, j], dp=partner)

        def arrived(j):
            forward(0, j).wait_recv()

        if not last:
            def use(t, value, it=it):
                return value + lax.dot_general(pair[t], fac[it, 2 * t + core], NT, preferred_element_type=F32)

            def step(s, value):
                t = xor(chip, s, chips)
                arrived(2 * t + core)
                return use(t, value)

            value = use(chip, jnp.zeros((rows, rank), F32))
        else:
            def use(j, value, it=it):
                approx = jnp.dot(low_t, fac[it, j], preferred_element_type=F32)
                residual = (comb[j].astype(F32) - approx).astype(BF16)
                g_buf[j] = residual
                pltpu.make_async_copy(g_buf.at[j], columns(new_error, j), o_sem.at[j]).start()
                wide = residual.astype(F32)
                squares = jnp.sum((wide * wide).reshape(rows // GROUP, GROUP, share), axis=0)
                for h in range(share // LANES):
                    value = value + squares[:, LANES * h : LANES * (h + 1)]
                return value

            def step(s, value):
                t = xor(chip, s, chips)
                arrived(2 * t + core)
                forward(s, 2 * t + core).start()
                value = use(2 * t + core, value)
                arrived(2 * t + 1 - core)
                return use(2 * t + 1 - core, value)

            value = use(me, jnp.zeros(n1.shape[1:], F32))
            arrived(partner)
            value = use(partner, value)

        total = lax.fori_loop(1, chips, step, value)

    n1[me] = total
    copies = [
        send(n1.at[me], n1.at[me], n1_ss.at[s], n1_rs.at[s], dp=lax.rem(me + s, n)) for s in range(1, n)
    ]
    for copy in copies:
        copy.start()
    for copy in copies:
        copy.wait_recv()
    pending += copies
    total = n1[0]
    for j in range(1, n):
        total = total + n1[j]
    n2[place] = total
    copies = [
        send(n2.at[place], n2.at[place], n2_ss.at[s], n2_rs.at[s], expert=lax.rem(place + s, experts))
        for s in range(1, experts)
    ]
    for copy in copies:
        copy.start()
    for copy in copies:
        copy.wait_recv()
    pending += copies
    total = n2[0]
    for j in range(1, experts):
        total = total + n2[j]
    norm[...] = jnp.sqrt(jnp.sum(total, keepdims=True) / count)

    for copy in pending:
        copy.wait_send()
    for s in range(1, chips):
        forward(s, 2 * xor(chip, s, chips) + core).wait_send()
    for t in range(chips):
        hand_over(t).wait_send()
    for j in range(n):
        pltpu.make_async_copy(g_buf.at[j], columns(new_error, j), o_sem.at[j]).wait()


def hand_out_kernel(basis, q, new_error, basis_out, q_out, new_error_out, b_buf, q_buf, e_buf, in_sem, out_sem):
    parts = in_sem.shape[0] - 2
    height = new_error.shape[0] // parts

    def piece(ref, i):
        return ref.at[pl.ds(i * height, height), :]

    moves = [(piece(new_error, i), piece(e_buf, i), piece(new_error_out, i)) for i in range(parts)]
    moves += [(basis, b_buf, basis_out), (q, q_buf, q_out)]
    inward = [pltpu.make_async_copy(a, b, in_sem.at[i]) for i, (a, b, c) in enumerate(moves)]
    outward = [pltpu.make_async_copy(b, c, out_sem.at[i]) for i, (a, b, c) in enumerate(moves)]
    for copy in inward:
        copy.start()
    for copy, following in zip(inward, outward):
        copy.wait()
        following.start()
    for copy in outward:
        copy.wait()


def hand_out(*arrays):
    hbm = pl.BlockSpec(memory_space=pl.ANY)
    return pl.pallas_call(
        hand_out_kernel,
        out_shape=tuple(jax.ShapeDtypeStruct(a.shape, a.dtype) for a in arrays),
        in_specs=[hbm] * 3,
        out_specs=(hbm,) * 3,
        scratch_shapes=[pltpu.VMEM(a.shape, a.dtype) for a in arrays] + [pltpu.SemaphoreType.DMA((16 + 2,))] * 2,
        compiler_params=pltpu.CompilerParams(vmem_limit_bytes=60 * 2**20),
    )(*arrays)


def local(grad, error, q_init):
    n, experts = lax.axis_size("dp"), lax.axis_size("expert")
    rows, width = grad.shape[2:]
    rank = q_init.shape[1]
    share = width // n
    chips = n // 2
    count = rows * width * n * experts
    dma = pltpu.SemaphoreType.DMA
    vmem, hbm = pl.BlockSpec(memory_space=pltpu.VMEM), pl.BlockSpec(memory_space=pl.ANY)
    hop = pltpu.VMEM((ITERS, chips, rank, share), BF16)
    basis, q, new_error, norm = pl.pallas_call(
        functools.partial(kernel, n, experts, count),
        out_shape=(
            jax.ShapeDtypeStruct((rank, rows), F32),
            jax.ShapeDtypeStruct((rank, share), F32),
            jax.ShapeDtypeStruct((rows, width), BF16),
            jax.ShapeDtypeStruct((1, 1), F32),
        ),
        in_specs=[hbm, hbm, hbm],
        out_specs=(vmem, vmem, hbm, vmem),
        scratch_shapes=[
            pltpu.VMEM((n, rows, share), BF16),
            pltpu.VMEM((n, rows, share), BF16),
            pltpu.VMEM((n, rows, share), BF16),
            pltpu.VMEM((chips, rows, share), BF16),
            pltpu.VMEM((chips, rows, share), BF16),
            pltpu.VMEM((chips, rank, share), BF16),
            pltpu.VMEM((ITERS, n, rank, share), BF16),
            hop, hop,
            pltpu.VMEM((ITERS, rank, rows), F32),
            pltpu.VMEM((ITERS, rank, rows), F32),
            pltpu.VMEM((ITERS, chips, rank, rows), F32),
            pltpu.VMEM((n, GROUP, LANES), F32),
            pltpu.VMEM((experts, GROUP, LANES), F32),
            dma((n,)), dma((n,)), dma((chips,)), dma((n,)),
            dma((chips,)), dma((chips,)), dma((ITERS, chips)), dma((ITERS, chips)),
            dma((ITERS,)), dma((ITERS,)), dma((ITERS, chips)), dma((ITERS, chips)),
            dma((ITERS, chips)), dma((chips,)), dma((ITERS, n)),
            dma((n,)), dma((n,)), dma((experts,)), dma((experts,)),
        ],
        compiler_params=pltpu.CompilerParams(
            collective_id=0, has_side_effects=True, vmem_limit_bytes=56 * 2**20
        ),
        cost_estimate=pl.CostEstimate(
            flops=2 * 5 * rows * rank * width, bytes_accessed=6 * rows * width, transcendentals=0
        ),
    )(grad[0, 0], error[0, 0], q_init[0])
    basis, q, new_error = hand_out(basis, q, new_error)
    return (jnp.transpose(basis)[None], q[None], new_error[None, None], norm[0, 0])


def solution(mesh):
    placed = (P("expert", "dp", None, None), P("expert", "dp", None, None), P("expert", None, None))
    return jax.shard_map(
        local,
        mesh=mesh,
        in_specs=placed,
        out_specs=(
            P("expert", None, None),
            P("expert", None, "dp"),
            P("expert", "dp", None, None),
            P(),
        ),
        check_vma=False,
    )
```

```python
import functools

import jax
import jax.numpy as jnp
from jax import lax
from jax.experimental import pallas as pl
from jax.experimental.pallas import tpu as pltpu
from jax.sharding import PartitionSpec as P

ITERS = 2
MESH = pl.DeviceIdType.MESH
F32 = jnp.float32
BF16 = jnp.bfloat16
LANES = 128
GROUP = 8
NT = (((1,), (1,)), ((), ()))


def xor(a, b, size):
    out, bit = 0, 1
    while bit < size:
        out = out + bit * lax.rem(lax.div(a, bit) + lax.div(b, bit), 2)
        bit *= 2
    return out


def spread_row(tile, j):
    return jnp.broadcast_to(tile[j : j + 1, :], tile.shape)


def inverted(x):
    guess = pl.reciprocal(x, approx=True)
    for _ in range(2):
        guess = guess * (2.0 - x * guess)
    return guess


def orthonormal_rows(pt):
    rank, rows = pt.shape
    groups, halves = rank // GROUP, rows // LANES
    padded = jnp.concatenate([pt, jnp.zeros((LANES - rank, rows), F32)], axis=0)
    gram = lax.dot_general(pt, padded, NT, precision=lax.Precision.HIGHEST, preferred_element_type=F32)
    g = [gram[GROUP * i : GROUP * (i + 1), :] for i in range(groups)]
    x = [
        [pt[GROUP * i : GROUP * (i + 1), LANES * h : LANES * (h + 1)] for h in range(halves)]
        for i in range(groups)
    ]
    row_id = lax.broadcasted_iota(jnp.int32, (GROUP, LANES), 0)
    for b in range(groups):
        below = range(b, groups)
        col = [
            {i: jnp.broadcast_to(g[i][:, GROUP * b + j : GROUP * b + j + 1], (GROUP, LANES)) for i in below}
            for j in range(GROUP)
        ]
        entry = {(j, k): spread_row(col[k][b], j) for j in range(GROUP) for k in range(j, GROUP)}
        pivots = jnp.ones((GROUP, LANES), F32)
        for j in range(GROUP):
            pivot = entry[j, j]
            pivots = jnp.where(row_id == j, pivot, pivots)
            inverse = inverted(pivot)
            for k in range(j + 1, GROUP):
                ratio = entry[j, k] * inverse
                for l in range(k, GROUP):
                    entry[k, l] = entry[k, l] - ratio * entry[j, l]
            factor = {i: col[j][i] * inverse for i in below}
            factor[b] = jnp.where(row_id > j, factor[b], 0.0)
            for k in range(j + 1, GROUP):
                for i in below:
                    col[k][i] = col[k][i] - factor[i] * entry[j, k]
            for h in range(halves):
                row = spread_row(x[b][h], j)
                for i in below:
                    x[i][h] = x[i][h] - factor[i] * row
            if b + 1 < groups:
                row = spread_row(g[b], j)
                for i in below:
                    g[i] = g[i] - factor[i] * row
        scale = lax.rsqrt(pivots)
        for h in range(halves):
            x[b][h] = x[b][h] * scale
    return jnp.concatenate([jnp.concatenate(parts, axis=1) for parts in x], axis=0)


def kernel(
    n, experts, count,
    grad, error, q_init,
    basis, q_out, new_error, norm,
    g_buf, e_buf, comb, theirs, pair, fac0, fac,
    s2_send, s2_recv, p1, p1_recv, p2, n1, n2,
    g_sem, e_sem, q_sem, o_sem,
    s1_ss, s1_rs, s2_ss, s2_rs, p1_ss, p1_rs, p2_ss, p2_rs,
    ag_ss, fw_ss, ag_rs, n1_ss, n1_rs, n2_ss, n2_rs,
):
    me = lax.axis_index("dp")
    place = lax.axis_index("expert")
    chip, core = lax.div(me, 2), lax.rem(me, 2)
    partner = 2 * chip + 1 - core
    chips = n // 2
    rows, share, rank = comb.shape[1], comb.shape[2], fac0.shape[1]

    def send(src, dst, ssem, rsem, **where):
        return pltpu.make_async_remote_copy(
            src_ref=src, dst_ref=dst, send_sem=ssem, recv_sem=rsem, device_id=where, device_id_type=MESH
        )

    def columns(ref, j):
        return ref.at[:, pl.ds(pl.multiple_of(j * share, share), share)]

    def load(j):
        return (
            pltpu.make_async_copy(columns(grad, j), g_buf.at[j], g_sem.at[j]),
            pltpu.make_async_copy(columns(error, j), e_buf.at[j], e_sem.at[j]),
        )

    def load_factor(t):
        return pltpu.make_async_copy(columns(q_init, 2 * t + core), fac0.at[t], q_sem.at[t])

    def combine(j):
        for copy in load(j):
            copy.wait()
        comb[j] = (g_buf[j].astype(F32) + e_buf[j].astype(F32)).astype(BF16)

    def hand_over(t):
        return send(comb.at[2 * t + 1 - core], theirs.at[t], s1_ss.at[t], s1_rs.at[t], dp=partner)

    for t in range(chips):
        for copy in load(2 * t + 1 - core):
            copy.start()
    for t in range(chips):
        for copy in load(2 * t + core):
            copy.start()
        load_factor(t).start()

    barrier = pltpu.get_barrier_semaphore()
    for s in range(1, n):
        pl.semaphore_signal(barrier, inc=1, device_id={"dp": lax.rem(me + s, n)}, device_id_type=MESH)
    for s in range(1, experts):
        pl.semaphore_signal(
            barrier, inc=1, device_id={"expert": lax.rem(place + s, experts)}, device_id_type=MESH
        )

    combine(1 - core)
    pl.semaphore_wait(barrier, n - 1 + experts - 1)
    hand_over(0).start()

    def first(t, _):
        combine(2 * t + 1 - core)
        hand_over(t).start()
        return 0

    lax.fori_loop(1, chips, first, 0)

    def second(t, total):
        combine(2 * t + core)
        load_factor(t).wait()
        hand_over(t).wait_recv()
        pair[t] = (comb[2 * t + core].astype(F32) + theirs[t].astype(F32)).astype(BF16)
        return total + lax.dot_general(pair[t], fac0[t], NT, preferred_element_type=F32)

    total = lax.fori_loop(0, chips, second, jnp.zeros((rows, rank), F32))

    pending = []
    for it in range(ITERS):
        last = it == ITERS - 1
        p1[it] = jnp.transpose(total)
        copy = send(p1.at[it], p1_recv.at[it], p1_ss.at[it], p1_rs.at[it], dp=partner)
        copy.start()
        pending.append(copy)
        copy.wait_recv()
        p2[it, chip] = p1[it] + p1_recv[it]
        copies = []
        for s in range(chips - 1, 0, -1):
            copies.append(
                send(
                    p2.at[it, chip], p2.at[it, chip], p2_ss.at[it, s], p2_rs.at[it, s],
                    dp=2 * xor(chip, s, chips) + core,
                )
            )
            copies[-1].start()
        for copy in copies:
            copy.wait_recv()
        pending += copies
        pt = p2[it, 0]
        for t in range(1, chips):
            pt = pt + p2[it, t]
        pt = pt / n
        ortho = orthonormal_rows(pt)
        low = ortho.astype(BF16)

        second_hop = []
        for s in range(chips - 1, -1, -1):
            q = jnp.dot(low, pair[xor(chip, s, chips)], preferred_element_type=F32)
            if s:
                s2_send[it, s] = q.astype(BF16)
                second_hop.append(
                    send(
                        s2_send.at[it, s], s2_recv.at[it, s], s2_ss.at[it, s], s2_rs.at[it, s],
                        dp=2 * xor(chip, s, chips) + core,
                    )
                )
                second_hop[-1].start()
        if last:
            basis[...] = ortho
            low_t = jnp.transpose(ortho).astype(BF16)
        for copy in second_hop:
            copy.wait_recv()
        for s in range(1, chips):
            q = q + s2_recv[it, s].astype(F32)
        q = q / n
        pending += second_hop
        if last:
            q_out[...] = q
        fac[it, me] = q.astype(BF16)

        for s in range(chips - 1, -1 if last else 0, -1):
            target = partner if s == 0 else 2 * xor(chip, s, chips) + core
            copy = send(fac.at[it, me], fac.at[it, me], ag_ss.at[it, s], ag_rs.at[it, me], dp=target)
            copy.start()
            pending.append(copy)

        def forward(s, j, it=it):
            return send(fac.at[it, j], fac.at[it, j], fw_ss.at[s], ag_rs.at[it, j], dp=partner)

        def arrived(j):
            forward(0, j).wait_recv()

        if not last:
            def use(t, value, it=it):
                return value + lax.dot_general(pair[t], fac[it, 2 * t + core], NT, preferred_element_type=F32)

            def step(s, value):
                t = xor(chip, s, chips)
                arrived(2 * t + core)
                return use(t, value)

            value = use(chip, jnp.zeros((rows, rank), F32))
        else:
            def use(j, value, it=it):
                approx = jnp.dot(low_t, fac[it, j], preferred_element_type=F32)
                residual = (comb[j].astype(F32) - approx).astype(BF16)
                g_buf[j] = residual
                pltpu.make_async_copy(g_buf.at[j], columns(new_error, j), o_sem.at[j]).start()
                wide = residual.astype(F32)
                squares = jnp.sum((wide * wide).reshape(rows // GROUP, GROUP, share), axis=0)
                for h in range(share // LANES):
                    value = value + squares[:, LANES * h : LANES * (h + 1)]
                return value

            def step(s, value):
                t = xor(chip, s, chips)
                arrived(2 * t + core)
                forward(s, 2 * t + core).start()
                value = use(2 * t + core, value)
                arrived(2 * t + 1 - core)
                return use(2 * t + 1 - core, value)

            value = use(me, jnp.zeros(n1.shape[1:], F32))
            arrived(partner)
            value = use(partner, value)

        total = lax.fori_loop(1, chips, step, value)

    n1[me] = total
    copies = [
        send(n1.at[me], n1.at[me], n1_ss.at[s], n1_rs.at[s], dp=lax.rem(me + s, n)) for s in range(1, n)
    ]
    for copy in copies:
        copy.start()
    for copy in copies:
        copy.wait_recv()
    pending += copies
    total = n1[0]
    for j in range(1, n):
        total = total + n1[j]
    n2[place] = total
    copies = [
        send(n2.at[place], n2.at[place], n2_ss.at[s], n2_rs.at[s], expert=lax.rem(place + s, experts))
        for s in range(1, experts)
    ]
    for copy in copies:
        copy.start()
    for copy in copies:
        copy.wait_recv()
    pending += copies
    total = n2[0]
    for j in range(1, experts):
        total = total + n2[j]
    norm[...] = jnp.sqrt(jnp.sum(total, keepdims=True) / count)

    for copy in pending:
        copy.wait_send()
    for s in range(1, chips):
        forward(s, 2 * xor(chip, s, chips) + core).wait_send()
    for t in range(chips):
        hand_over(t).wait_send()
    for j in range(n):
        pltpu.make_async_copy(g_buf.at[j], columns(new_error, j), o_sem.at[j]).wait()


def hand_out_kernel(basis, q, new_error, basis_out, q_out, new_error_out, sem):
    parts = sem.shape[0] - 2
    height = new_error.shape[0] // parts

    def piece(ref, i):
        return ref.at[pl.ds(i * height, height), :]

    moves = [(piece(new_error, i), piece(new_error_out, i)) for i in range(parts)]
    moves += [(basis, basis_out), (q, q_out)]
    copies = [pltpu.make_async_copy(a, b, sem.at[i]) for i, (a, b) in enumerate(moves)]
    for copy in copies:
        copy.start()
    for copy in copies:
        copy.wait()


def hand_out(*arrays):
    hbm = pl.BlockSpec(memory_space=pl.ANY)
    return pl.pallas_call(
        hand_out_kernel,
        out_shape=tuple(jax.ShapeDtypeStruct(a.shape, a.dtype) for a in arrays),
        in_specs=[hbm] * 3,
        out_specs=(hbm,) * 3,
        scratch_shapes=[pltpu.SemaphoreType.DMA((16 + 2,))],
        compiler_params=pltpu.CompilerParams(vmem_limit_bytes=32 * 2**20),
    )(*arrays)


def local(grad, error, q_init):
    n, experts = lax.axis_size("dp"), lax.axis_size("expert")
    rows, width = grad.shape[2:]
    rank = q_init.shape[1]
    share = width // n
    chips = n // 2
    count = rows * width * n * experts
    dma = pltpu.SemaphoreType.DMA
    vmem, hbm = pl.BlockSpec(memory_space=pltpu.VMEM), pl.BlockSpec(memory_space=pl.ANY)
    hop = pltpu.VMEM((ITERS, chips, rank, share), BF16)
    basis, q, new_error, norm = pl.pallas_call(
        functools.partial(kernel, n, experts, count),
        out_shape=(
            jax.ShapeDtypeStruct((rank, rows), F32),
            jax.ShapeDtypeStruct((rank, share), F32),
            jax.ShapeDtypeStruct((rows, width), BF16),
            jax.ShapeDtypeStruct((1, 1), F32),
        ),
        in_specs=[hbm, hbm, hbm],
        out_specs=(vmem, vmem, hbm, vmem),
        scratch_shapes=[
            pltpu.VMEM((n, rows, share), BF16),
            pltpu.VMEM((n, rows, share), BF16),
            pltpu.VMEM((n, rows, share), BF16),
            pltpu.VMEM((chips, rows, share), BF16),
            pltpu.VMEM((chips, rows, share), BF16),
            pltpu.VMEM((chips, rank, share), BF16),
            pltpu.VMEM((ITERS, n, rank, share), BF16),
            hop, hop,
            pltpu.VMEM((ITERS, rank, rows), F32),
            pltpu.VMEM((ITERS, rank, rows), F32),
            pltpu.VMEM((ITERS, chips, rank, rows), F32),
            pltpu.VMEM((n, GROUP, LANES), F32),
            pltpu.VMEM((experts, GROUP, LANES), F32),
            dma((n,)), dma((n,)), dma((chips,)), dma((n,)),
            dma((chips,)), dma((chips,)), dma((ITERS, chips)), dma((ITERS, chips)),
            dma((ITERS,)), dma((ITERS,)), dma((ITERS, chips)), dma((ITERS, chips)),
            dma((ITERS, chips)), dma((chips,)), dma((ITERS, n)),
            dma((n,)), dma((n,)), dma((experts,)), dma((experts,)),
        ],
        compiler_params=pltpu.CompilerParams(
            collective_id=0, has_side_effects=True, vmem_limit_bytes=49 * 2**20
        ),
        cost_estimate=pl.CostEstimate(
            flops=2 * 5 * rows * rank * width, bytes_accessed=6 * rows * width, transcendentals=0
        ),
    )(grad[0, 0], error[0, 0], q_init[0])
    basis, q, new_error = hand_out(basis, q, new_error)
    return (jnp.transpose(basis)[None], q[None], new_error[None, None], norm[0, 0])


def solution(mesh):
    placed = (P("expert", "dp", None, None), P("expert", "dp", None, None), P("expert", None, None))
    return jax.shard_map(
        local,
        mesh=mesh,
        in_specs=placed,
        out_specs=(
            P("expert", None, None),
            P("expert", None, "dp"),
            P("expert", "dp", None, None),
            P(),
        ),
        check_vma=False,
    )
```

```python
import functools

import jax
import jax.numpy as jnp
from jax import lax
from jax.experimental import pallas as pl
from jax.experimental.pallas import tpu as pltpu
from jax.sharding import PartitionSpec as P

ITERS = 2
MESH = pl.DeviceIdType.MESH
F32 = jnp.float32
BF16 = jnp.bfloat16
LANES = 128
GROUP = 8
NT = (((1,), (1,)), ((), ()))


def xor(a, b, size):
    out, bit = 0, 1
    while bit < size:
        out = out + bit * lax.rem(lax.div(a, bit) + lax.div(b, bit), 2)
        bit *= 2
    return out


def spread_row(tile, j):
    return jnp.broadcast_to(tile[j : j + 1, :], tile.shape)


def orthonormal_rows(pt):
    rank, rows = pt.shape
    groups, halves = rank // GROUP, rows // LANES
    padded = jnp.concatenate([pt, jnp.zeros((LANES - rank, rows), F32)], axis=0)
    gram = lax.dot_general(pt, padded, NT, precision=lax.Precision.HIGHEST, preferred_element_type=F32)
    g = [gram[GROUP * i : GROUP * (i + 1), :] for i in range(groups)]
    x = [
        [pt[GROUP * i : GROUP * (i + 1), LANES * h : LANES * (h + 1)] for h in range(halves)]
        for i in range(groups)
    ]
    row_id = lax.broadcasted_iota(jnp.int32, (GROUP, LANES), 0)
    for b in range(groups):
        below = range(b, groups)
        col = [
            {i: jnp.broadcast_to(g[i][:, GROUP * b + j : GROUP * b + j + 1], (GROUP, LANES)) for i in below}
            for j in range(GROUP)
        ]
        pivots = jnp.ones((GROUP, LANES), F32)
        for j in range(GROUP):
            pivot = spread_row(col[j][b], j)
            pivots = jnp.where(row_id == j, pivot, pivots)
            inverse = 1.0 / pivot
            factor = {i: col[j][i] * inverse for i in below}
            factor[b] = jnp.where(row_id > j, factor[b], 0.0)
            for k in range(j + 1, GROUP):
                row = spread_row(col[k][b], j)
                for i in below:
                    col[k][i] = col[k][i] - factor[i] * row
            for h in range(halves):
                row = spread_row(x[b][h], j)
                for i in below:
                    x[i][h] = x[i][h] - factor[i] * row
            if b + 1 < groups:
                row = spread_row(g[b], j)
                for i in below:
                    g[i] = g[i] - factor[i] * row
        scale = lax.rsqrt(pivots)
        for h in range(halves):
            x[b][h] = x[b][h] * scale
    return jnp.concatenate([jnp.concatenate(parts, axis=1) for parts in x], axis=0)


def kernel(
    n, experts, count,
    grad, error, q_init,
    basis, q_out, new_error, norm,
    g_buf, e_buf, comb, theirs, pair, fac0, fac,
    s2_send, s2_recv, p, n1, n2,
    g_sem, e_sem, q_sem, o_sem,
    s1_ss, s1_rs, s2_ss, s2_rs, p_ss, p_rs,
    ag_ss, fw_ss, ag_rs, n1_ss, n1_rs, n2_ss, n2_rs,
):
    me = lax.axis_index("dp")
    place = lax.axis_index("expert")
    chip, core = lax.div(me, 2), lax.rem(me, 2)
    partner = 2 * chip + 1 - core
    chips = n // 2
    rows, share, rank = comb.shape[1], comb.shape[2], fac0.shape[1]

    def send(src, dst, ssem, rsem, **where):
        return pltpu.make_async_remote_copy(
            src_ref=src, dst_ref=dst, send_sem=ssem, recv_sem=rsem, device_id=where, device_id_type=MESH
        )

    def columns(ref, j):
        return ref.at[:, pl.ds(pl.multiple_of(j * share, share), share)]

    def load(j):
        return (
            pltpu.make_async_copy(columns(grad, j), g_buf.at[j], g_sem.at[j]),
            pltpu.make_async_copy(columns(error, j), e_buf.at[j], e_sem.at[j]),
            pltpu.make_async_copy(columns(q_init, j), fac0.at[j], q_sem.at[j]),
        )

    def combine(j, total):
        for copy in load(j):
            copy.wait()
        comb[j] = (g_buf[j].astype(F32) + e_buf[j].astype(F32)).astype(BF16)
        return total + lax.dot_general(comb[j], fac0[j], NT, preferred_element_type=F32)

    def hand_over(t):
        return send(comb.at[2 * t + 1 - core], theirs.at[t], s1_ss.at[t], s1_rs.at[t], dp=partner)

    for t in range(chips):
        for copy in load(2 * t + 1 - core):
            copy.start()
    for t in range(chips):
        for copy in load(2 * t + core):
            copy.start()

    barrier = pltpu.get_barrier_semaphore()
    for s in range(1, n):
        pl.semaphore_signal(barrier, inc=1, device_id={"dp": lax.rem(me + s, n)}, device_id_type=MESH)
    for s in range(1, experts):
        pl.semaphore_signal(
            barrier, inc=1, device_id={"expert": lax.rem(place + s, experts)}, device_id_type=MESH
        )

    total = combine(1 - core, jnp.zeros((rows, rank), F32))
    pl.semaphore_wait(barrier, n - 1 + experts - 1)
    hand_over(0).start()

    def first(t, total):
        total = combine(2 * t + 1 - core, total)
        hand_over(t).start()
        return total

    total = lax.fori_loop(1, chips, first, total)
    total = lax.fori_loop(0, chips, lambda t, total: combine(2 * t + core, total), total)

    def add_pair(t, _):
        hand_over(t).wait_recv()
        pair[t] = (comb[2 * t + core].astype(F32) + theirs[t].astype(F32)).astype(BF16)
        return 0

    pending = []
    for it in range(ITERS):
        last = it == ITERS - 1
        p[it, me] = jnp.transpose(total).astype(BF16)
        copies = []
        for s in range(n - 1, 0, -1):
            copies.append(
                send(p.at[it, me], p.at[it, me], p_ss.at[it, s], p_rs.at[it, s], dp=xor(me, s, n))
            )
            copies[-1].start()
        if it == 0:
            lax.fori_loop(0, chips, add_pair, 0)
        for copy in copies:
            copy.wait_recv()
        pending += copies
        pt = p[it, 0].astype(F32)
        for j in range(1, n):
            pt = pt + p[it, j].astype(F32)
        pt = pt / n
        ortho = orthonormal_rows(pt)
        low = ortho.astype(BF16)

        second_hop = []
        for s in range(chips - 1, -1, -1):
            q = jnp.dot(low, pair[xor(chip, s, chips)], preferred_element_type=F32)
            if s:
                s2_send[it, s] = q.astype(BF16)
                second_hop.append(
                    send(
                        s2_send.at[it, s], s2_recv.at[it, s], s2_ss.at[it, s], s2_rs.at[it, s],
                        dp=2 * xor(chip, s, chips) + core,
                    )
                )
                second_hop[-1].start()
        if last:
            basis[...] = ortho
            low_t = jnp.transpose(ortho).astype(BF16)
        for copy in second_hop:
            copy.wait_recv()
        for s in range(1, chips):
            q = q + s2_recv[it, s].astype(F32)
        q = q / n
        pending += second_hop
        if last:
            q_out[...] = q
        fac[it, me] = q.astype(BF16)

        for s in range(chips - 1, -1 if last else 0, -1):
            target = partner if s == 0 else 2 * xor(chip, s, chips) + core
            copy = send(fac.at[it, me], fac.at[it, me], ag_ss.at[it, s], ag_rs.at[it, me], dp=target)
            copy.start()
            pending.append(copy)

        def forward(s, j, it=it):
            return send(fac.at[it, j], fac.at[it, j], fw_ss.at[s], ag_rs.at[it, j], dp=partner)

        def arrived(j):
            forward(0, j).wait_recv()

        if not last:
            def use(t, value, it=it):
                return value + lax.dot_general(pair[t], fac[it, 2 * t + core], NT, preferred_element_type=F32)

            def step(s, value):
                t = xor(chip, s, chips)
                arrived(2 * t + core)
                return use(t, value)

            value = use(chip, jnp.zeros((rows, rank), F32))
        else:
            def use(j, value, it=it):
                approx = jnp.dot(low_t, fac[it, j], preferred_element_type=F32)
                residual = (comb[j].astype(F32) - approx).astype(BF16)
                g_buf[j] = residual
                pltpu.make_async_copy(g_buf.at[j], columns(new_error, j), o_sem.at[j]).start()
                wide = residual.astype(F32)
                squares = jnp.sum((wide * wide).reshape(rows // GROUP, GROUP, share), axis=0)
                for h in range(share // LANES):
                    value = value + squares[:, LANES * h : LANES * (h + 1)]
                return value

            def step(s, value):
                t = xor(chip, s, chips)
                arrived(2 * t + core)
                forward(s, 2 * t + core).start()
                value = use(2 * t + core, value)
                arrived(2 * t + 1 - core)
                return use(2 * t + 1 - core, value)

            value = use(me, jnp.zeros(n1.shape[1:], F32))
            arrived(partner)
            value = use(partner, value)

        total = lax.fori_loop(1, chips, step, value)

    n1[me] = total
    copies = [
        send(n1.at[me], n1.at[me], n1_ss.at[s], n1_rs.at[s], dp=lax.rem(me + s, n)) for s in range(1, n)
    ]
    for copy in copies:
        copy.start()
    for copy in copies:
        copy.wait_recv()
    pending += copies
    total = n1[0]
    for j in range(1, n):
        total = total + n1[j]
    n2[place] = total
    copies = [
        send(n2.at[place], n2.at[place], n2_ss.at[s], n2_rs.at[s], expert=lax.rem(place + s, experts))
        for s in range(1, experts)
    ]
    for copy in copies:
        copy.start()
    for copy in copies:
        copy.wait_recv()
    pending += copies
    total = n2[0]
    for j in range(1, experts):
        total = total + n2[j]
    norm[...] = jnp.sqrt(jnp.sum(total, keepdims=True) / count)

    for copy in pending:
        copy.wait_send()
    for s in range(1, chips):
        forward(s, 2 * xor(chip, s, chips) + core).wait_send()
    for t in range(chips):
        hand_over(t).wait_send()
    for j in range(n):
        pltpu.make_async_copy(g_buf.at[j], columns(new_error, j), o_sem.at[j]).wait()


def hand_out_kernel(basis, q, new_error, basis_out, q_out, new_error_out, sem):
    parts = sem.shape[0] - 2
    height = new_error.shape[0] // parts

    def piece(ref, i):
        return ref.at[pl.ds(i * height, height), :]

    moves = [(piece(new_error, i), piece(new_error_out, i)) for i in range(parts)]
    moves += [(basis, basis_out), (q, q_out)]
    copies = [pltpu.make_async_copy(a, b, sem.at[i]) for i, (a, b) in enumerate(moves)]
    for copy in copies:
        copy.start()
    for copy in copies:
        copy.wait()


def hand_out(*arrays):
    hbm = pl.BlockSpec(memory_space=pl.ANY)
    return pl.pallas_call(
        hand_out_kernel,
        out_shape=tuple(jax.ShapeDtypeStruct(a.shape, a.dtype) for a in arrays),
        in_specs=[hbm] * 3,
        out_specs=(hbm,) * 3,
        scratch_shapes=[pltpu.SemaphoreType.DMA((16 + 2,))],
        compiler_params=pltpu.CompilerParams(vmem_limit_bytes=32 * 2**20),
    )(*arrays)


def local(grad, error, q_init):
    n, experts = lax.axis_size("dp"), lax.axis_size("expert")
    rows, width = grad.shape[2:]
    rank = q_init.shape[1]
    share = width // n
    chips = n // 2
    count = rows * width * n * experts
    dma = pltpu.SemaphoreType.DMA
    vmem, hbm = pl.BlockSpec(memory_space=pltpu.VMEM), pl.BlockSpec(memory_space=pl.ANY)
    hop = pltpu.VMEM((ITERS, chips, rank, share), BF16)
    basis, q, new_error, norm = pl.pallas_call(
        functools.partial(kernel, n, experts, count),
        out_shape=(
            jax.ShapeDtypeStruct((rank, rows), F32),
            jax.ShapeDtypeStruct((rank, share), F32),
            jax.ShapeDtypeStruct((rows, width), BF16),
            jax.ShapeDtypeStruct((1, 1), F32),
        ),
        in_specs=[hbm, hbm, hbm],
        out_specs=(vmem, vmem, hbm, vmem),
        scratch_shapes=[
            pltpu.VMEM((n, rows, share), BF16),
            pltpu.VMEM((n, rows, share), BF16),
            pltpu.VMEM((n, rows, share), BF16),
            pltpu.VMEM((chips, rows, share), BF16),
            pltpu.VMEM((chips, rows, share), BF16),
            pltpu.VMEM((n, rank, share), BF16),
            pltpu.VMEM((ITERS, n, rank, share), BF16),
            hop, hop,
            pltpu.VMEM((ITERS, n, rank, rows), BF16),
            pltpu.VMEM((n, GROUP, LANES), F32),
            pltpu.VMEM((experts, GROUP, LANES), F32),
            dma((n,)), dma((n,)), dma((n,)), dma((n,)),
            dma((chips,)), dma((chips,)), dma((ITERS, chips)), dma((ITERS, chips)),
            dma((ITERS, n)), dma((ITERS, n)),
            dma((ITERS, chips)), dma((chips,)), dma((ITERS, n)),
            dma((n,)), dma((n,)), dma((experts,)), dma((experts,)),
        ],
        compiler_params=pltpu.CompilerParams(
            collective_id=0, has_side_effects=True, vmem_limit_bytes=49 * 2**20
        ),
        cost_estimate=pl.CostEstimate(
            flops=2 * 5 * rows * rank * width, bytes_accessed=6 * rows * width, transcendentals=0
        ),
    )(grad[0, 0], error[0, 0], q_init[0])
    basis, q, new_error = hand_out(basis, q, new_error)
    return (jnp.transpose(basis)[None], q[None], new_error[None, None], norm[0, 0])


def solution(mesh):
    placed = (P("expert", "dp", None, None), P("expert", "dp", None, None), P("expert", None, None))
    return jax.shard_map(
        local,
        mesh=mesh,
        in_specs=placed,
        out_specs=(
            P("expert", None, None),
            P("expert", None, "dp"),
            P("expert", "dp", None, None),
            P(),
        ),
        check_vma=False,
    )
```

```python
import functools

import jax
import jax.numpy as jnp
from jax import lax
from jax.experimental import pallas as pl
from jax.experimental.pallas import tpu as pltpu
from jax.sharding import PartitionSpec as P

ITERS = 2
MESH = pl.DeviceIdType.MESH
F32 = jnp.float32
BF16 = jnp.bfloat16
LANES = 128
GROUP = 8
NT = (((1,), (1,)), ((), ()))


def xor(a, b, size):
    out, bit = 0, 1
    while bit < size:
        out = out + bit * lax.rem(lax.div(a, bit) + lax.div(b, bit), 2)
        bit *= 2
    return out


def spread_row(tile, j):
    return jnp.broadcast_to(tile[j : j + 1, :], tile.shape)


def orthonormal_rows(pt):
    rank, rows = pt.shape
    groups = rank // GROUP
    padded = jnp.concatenate([pt, jnp.zeros((LANES - rank, rows), F32)], axis=0)
    gram = lax.dot_general(pt, padded, NT, precision=lax.Precision.HIGHEST, preferred_element_type=F32)
    lane = lax.broadcasted_iota(jnp.int32, (rank, LANES), 1)
    line = lax.broadcasted_iota(jnp.int32, (rank, LANES), 0)
    both = jnp.where(lane == line + rank, 1.0, gram)
    g = [both[GROUP * i : GROUP * (i + 1), :] for i in range(groups)]
    row_id = lax.broadcasted_iota(jnp.int32, (GROUP, LANES), 0)
    for b in range(groups):
        below = range(b, groups)
        col = [
            {i: jnp.broadcast_to(g[i][:, GROUP * b + j : GROUP * b + j + 1], (GROUP, LANES)) for i in below}
            for j in range(GROUP)
        ]
        pivots = jnp.ones((GROUP, LANES), F32)
        for j in range(GROUP):
            pivot = spread_row(col[j][b], j)
            pivots = jnp.where(row_id == j, pivot, pivots)
            inverse = 1.0 / pivot
            factor = {i: col[j][i] * inverse for i in below}
            factor[b] = jnp.where(row_id > j, factor[b], 0.0)
            for k in range(j + 1, GROUP):
                row = spread_row(col[k][b], j)
                for i in below:
                    col[k][i] = col[k][i] - factor[i] * row
            row = spread_row(g[b], j)
            for i in below:
                g[i] = g[i] - factor[i] * row
        g[b] = g[b] * lax.rsqrt(pivots)
    solver = jnp.where(lane >= rank, jnp.concatenate(g, axis=0), 0.0)
    padded = jnp.concatenate(
        [jnp.zeros((rank, rows), F32), pt, jnp.zeros((LANES - 2 * rank, rows), F32)], axis=0
    )
    return jnp.dot(solver, padded, precision=lax.Precision.HIGHEST, preferred_element_type=F32)


def kernel(
    n, experts, count,
    grad, error, q_init,
    basis, q_out, new_error, norm,
    g_buf, e_buf, comb, theirs, pair, fac0, fac,
    s2_send, s2_recv, p, n1, n2,
    g_sem, e_sem, q_sem, o_sem,
    s1_ss, s1_rs, s2_ss, s2_rs, p_ss, p_rs,
    ag_ss, fw_ss, ag_rs, n1_ss, n1_rs, n2_ss, n2_rs,
):
    me = lax.axis_index("dp")
    place = lax.axis_index("expert")
    chip, core = lax.div(me, 2), lax.rem(me, 2)
    partner = 2 * chip + 1 - core
    chips = n // 2
    rows, share, rank = comb.shape[1], comb.shape[2], fac0.shape[1]

    def send(src, dst, ssem, rsem, **where):
        return pltpu.make_async_remote_copy(
            src_ref=src, dst_ref=dst, send_sem=ssem, recv_sem=rsem, device_id=where, device_id_type=MESH
        )

    def columns(ref, j):
        return ref.at[:, pl.ds(pl.multiple_of(j * share, share), share)]

    def load(j):
        return (
            pltpu.make_async_copy(columns(grad, j), g_buf.at[j], g_sem.at[j]),
            pltpu.make_async_copy(columns(error, j), e_buf.at[j], e_sem.at[j]),
            pltpu.make_async_copy(columns(q_init, j), fac0.at[j], q_sem.at[j]),
        )

    def combine(j, total):
        for copy in load(j):
            copy.wait()
        comb[j] = (g_buf[j].astype(F32) + e_buf[j].astype(F32)).astype(BF16)
        return total + lax.dot_general(comb[j], fac0[j], NT, preferred_element_type=F32)

    def hand_over(t):
        return send(comb.at[2 * t + 1 - core], theirs.at[t], s1_ss.at[t], s1_rs.at[t], dp=partner)

    for t in range(chips):
        for copy in load(2 * t + 1 - core):
            copy.start()
    for t in range(chips):
        for copy in load(2 * t + core):
            copy.start()

    barrier = pltpu.get_barrier_semaphore()
    for s in range(1, n):
        pl.semaphore_signal(barrier, inc=1, device_id={"dp": lax.rem(me + s, n)}, device_id_type=MESH)
    for s in range(1, experts):
        pl.semaphore_signal(
            barrier, inc=1, device_id={"expert": lax.rem(place + s, experts)}, device_id_type=MESH
        )

    total = combine(1 - core, jnp.zeros((rows, rank), F32))
    pl.semaphore_wait(barrier, n - 1 + experts - 1)
    hand_over(0).start()

    def first(t, total):
        total = combine(2 * t + 1 - core, total)
        hand_over(t).start()
        return total

    total = lax.fori_loop(1, chips, first, total)
    total = lax.fori_loop(0, chips, lambda t, total: combine(2 * t + core, total), total)

    def add_pair(t, _):
        hand_over(t).wait_recv()
        pair[t] = (comb[2 * t + core].astype(F32) + theirs[t].astype(F32)).astype(BF16)
        return 0

    pending = []
    for it in range(ITERS):
        last = it == ITERS - 1
        p[it, me] = jnp.transpose(total).astype(BF16)
        copies = []
        for s in range(n - 1, 0, -1):
            copies.append(
                send(p.at[it, me], p.at[it, me], p_ss.at[it, s], p_rs.at[it, s], dp=xor(me, s, n))
            )
            copies[-1].start()
        if it == 0:
            lax.fori_loop(0, chips, add_pair, 0)
        for copy in copies:
            copy.wait_recv()
        pending += copies
        pt = p[it, 0].astype(F32)
        for j in range(1, n):
            pt = pt + p[it, j].astype(F32)
        pt = pt / n
        ortho = orthonormal_rows(pt)
        low = ortho.astype(BF16)

        second_hop = []
        for s in range(chips - 1, -1, -1):
            q = jnp.dot(low, pair[xor(chip, s, chips)], preferred_element_type=F32)
            if s:
                s2_send[it, s] = q.astype(BF16)
                second_hop.append(
                    send(
                        s2_send.at[it, s], s2_recv.at[it, s], s2_ss.at[it, s], s2_rs.at[it, s],
                        dp=2 * xor(chip, s, chips) + core,
                    )
                )
                second_hop[-1].start()
        if last:
            basis[...] = ortho
            low_t = jnp.transpose(ortho).astype(BF16)
        for copy in second_hop:
            copy.wait_recv()
        for s in range(1, chips):
            q = q + s2_recv[it, s].astype(F32)
        q = q / n
        pending += second_hop
        if last:
            q_out[...] = q
        fac[it, me] = q.astype(BF16)

        for s in range(chips - 1, -1 if last else 0, -1):
            target = partner if s == 0 else 2 * xor(chip, s, chips) + core
            copy = send(fac.at[it, me], fac.at[it, me], ag_ss.at[it, s], ag_rs.at[it, me], dp=target)
            copy.start()
            pending.append(copy)

        def forward(s, j, it=it):
            return send(fac.at[it, j], fac.at[it, j], fw_ss.at[s], ag_rs.at[it, j], dp=partner)

        def arrived(j):
            forward(0, j).wait_recv()

        if not last:
            def use(t, value, it=it):
                return value + lax.dot_general(pair[t], fac[it, 2 * t + core], NT, preferred_element_type=F32)

            def step(s, value):
                t = xor(chip, s, chips)
                arrived(2 * t + core)
                return use(t, value)

            value = use(chip, jnp.zeros((rows, rank), F32))
        else:
            def use(j, value, it=it):
                approx = jnp.dot(low_t, fac[it, j], preferred_element_type=F32)
                residual = (comb[j].astype(F32) - approx).astype(BF16)
                g_buf[j] = residual
                pltpu.make_async_copy(g_buf.at[j], columns(new_error, j), o_sem.at[j]).start()
                wide = residual.astype(F32)
                squares = jnp.sum((wide * wide).reshape(rows // GROUP, GROUP, share), axis=0)
                for h in range(share // LANES):
                    value = value + squares[:, LANES * h : LANES * (h + 1)]
                return value

            def step(s, value):
                t = xor(chip, s, chips)
                arrived(2 * t + core)
                forward(s, 2 * t + core).start()
                value = use(2 * t + core, value)
                arrived(2 * t + 1 - core)
                return use(2 * t + 1 - core, value)

            value = use(me, jnp.zeros(n1.shape[1:], F32))
            arrived(partner)
            value = use(partner, value)

        total = lax.fori_loop(1, chips, step, value)

    n1[me] = total
    copies = [
        send(n1.at[me], n1.at[me], n1_ss.at[s], n1_rs.at[s], dp=lax.rem(me + s, n)) for s in range(1, n)
    ]
    for copy in copies:
        copy.start()
    for copy in copies:
        copy.wait_recv()
    pending += copies
    total = n1[0]
    for j in range(1, n):
        total = total + n1[j]
    n2[place] = total
    copies = [
        send(n2.at[place], n2.at[place], n2_ss.at[s], n2_rs.at[s], expert=lax.rem(place + s, experts))
        for s in range(1, experts)
    ]
    for copy in copies:
        copy.start()
    for copy in copies:
        copy.wait_recv()
    pending += copies
    total = n2[0]
    for j in range(1, experts):
        total = total + n2[j]
    norm[...] = jnp.sqrt(jnp.sum(total, keepdims=True) / count)

    for copy in pending:
        copy.wait_send()
    for s in range(1, chips):
        forward(s, 2 * xor(chip, s, chips) + core).wait_send()
    for t in range(chips):
        hand_over(t).wait_send()
    for j in range(n):
        pltpu.make_async_copy(g_buf.at[j], columns(new_error, j), o_sem.at[j]).wait()


def hand_out_kernel(basis, q, new_error, basis_out, q_out, new_error_out, sem):
    parts = sem.shape[0] - 2
    height = new_error.shape[0] // parts

    def piece(ref, i):
        return ref.at[pl.ds(i * height, height), :]

    moves = [(piece(new_error, i), piece(new_error_out, i)) for i in range(parts)]
    moves += [(basis, basis_out), (q, q_out)]
    copies = [pltpu.make_async_copy(a, b, sem.at[i]) for i, (a, b) in enumerate(moves)]
    for copy in copies:
        copy.start()
    for copy in copies:
        copy.wait()


def hand_out(*arrays):
    hbm = pl.BlockSpec(memory_space=pl.ANY)
    return pl.pallas_call(
        hand_out_kernel,
        out_shape=tuple(jax.ShapeDtypeStruct(a.shape, a.dtype) for a in arrays),
        in_specs=[hbm] * 3,
        out_specs=(hbm,) * 3,
        scratch_shapes=[pltpu.SemaphoreType.DMA((16 + 2,))],
        compiler_params=pltpu.CompilerParams(vmem_limit_bytes=32 * 2**20),
    )(*arrays)


def local(grad, error, q_init):
    n, experts = lax.axis_size("dp"), lax.axis_size("expert")
    rows, width = grad.shape[2:]
    rank = q_init.shape[1]
    share = width // n
    chips = n // 2
    count = rows * width * n * experts
    dma = pltpu.SemaphoreType.DMA
    vmem, hbm = pl.BlockSpec(memory_space=pltpu.VMEM), pl.BlockSpec(memory_space=pl.ANY)
    hop = pltpu.VMEM((ITERS, chips, rank, share), BF16)
    basis, q, new_error, norm = pl.pallas_call(
        functools.partial(kernel, n, experts, count),
        out_shape=(
            jax.ShapeDtypeStruct((rank, rows), F32),
            jax.ShapeDtypeStruct((rank, share), F32),
            jax.ShapeDtypeStruct((rows, width), BF16),
            jax.ShapeDtypeStruct((1, 1), F32),
        ),
        in_specs=[hbm, hbm, hbm],
        out_specs=(vmem, vmem, hbm, vmem),
        scratch_shapes=[
            pltpu.VMEM((n, rows, share), BF16),
            pltpu.VMEM((n, rows, share), BF16),
            pltpu.VMEM((n, rows, share), BF16),
            pltpu.VMEM((chips, rows, share), BF16),
            pltpu.VMEM((chips, rows, share), BF16),
            pltpu.VMEM((n, rank, share), BF16),
            pltpu.VMEM((ITERS, n, rank, share), BF16),
            hop, hop,
            pltpu.VMEM((ITERS, n, rank, rows), BF16),
            pltpu.VMEM((n, GROUP, LANES), F32),
            pltpu.VMEM((experts, GROUP, LANES), F32),
            dma((n,)), dma((n,)), dma((n,)), dma((n,)),
            dma((chips,)), dma((chips,)), dma((ITERS, chips)), dma((ITERS, chips)),
            dma((ITERS, n)), dma((ITERS, n)),
            dma((ITERS, chips)), dma((chips,)), dma((ITERS, n)),
            dma((n,)), dma((n,)), dma((experts,)), dma((experts,)),
        ],
        compiler_params=pltpu.CompilerParams(
            collective_id=0, has_side_effects=True, vmem_limit_bytes=49 * 2**20
        ),
        cost_estimate=pl.CostEstimate(
            flops=2 * 5 * rows * rank * width, bytes_accessed=6 * rows * width, transcendentals=0
        ),
    )(grad[0, 0], error[0, 0], q_init[0])
    basis, q, new_error = hand_out(basis, q, new_error)
    return (jnp.transpose(basis)[None], q[None], new_error[None, None], norm[0, 0])


def solution(mesh):
    placed = (P("expert", "dp", None, None), P("expert", "dp", None, None), P("expert", None, None))
    return jax.shard_map(
        local,
        mesh=mesh,
        in_specs=placed,
        out_specs=(
            P("expert", None, None),
            P("expert", None, "dp"),
            P("expert", "dp", None, None),
            P(),
        ),
        check_vma=False,
    )
```

```python
import functools

import jax
import jax.numpy as jnp
from jax import lax
from jax.experimental import pallas as pl
from jax.experimental.pallas import tpu as pltpu
from jax.sharding import PartitionSpec as P

ITERS = 2
MESH = pl.DeviceIdType.MESH
F32 = jnp.float32
BF16 = jnp.bfloat16
LANES = 128
GROUP = 8
HALF = 16
NT = (((1,), (1,)), ((), ()))


def xor(a, b, size):
    out, bit = 0, 1
    while bit < size:
        out = out + bit * lax.rem(lax.div(a, bit) + lax.div(b, bit), 2)
        bit *= 2
    return out


def spread_row(tile, j):
    return jnp.broadcast_to(tile[j : j + 1, :], tile.shape)


def orthonormal_rows(pt):
    rank, rows = pt.shape
    groups, halves = rank // GROUP, rows // LANES
    padded = jnp.concatenate([pt, jnp.zeros((LANES - rank, rows), F32)], axis=0)
    gram = lax.dot_general(pt, padded, NT, precision=lax.Precision.HIGHEST, preferred_element_type=F32)
    g = [gram[GROUP * i : GROUP * (i + 1), :] for i in range(groups)]
    x = [
        [pt[GROUP * i : GROUP * (i + 1), LANES * h : LANES * (h + 1)] for h in range(halves)]
        for i in range(groups)
    ]
    row_id = lax.broadcasted_iota(jnp.int32, (GROUP, LANES), 0)
    for b in range(groups):
        below = range(b, groups)
        col = [
            {i: jnp.broadcast_to(g[i][:, GROUP * b + j : GROUP * b + j + 1], (GROUP, LANES)) for i in below}
            for j in range(GROUP)
        ]
        pivots = jnp.ones((GROUP, LANES), F32)
        for j in range(GROUP):
            pivot = spread_row(col[j][b], j)
            pivots = jnp.where(row_id == j, pivot, pivots)
            inverse = 1.0 / pivot
            factor = {i: col[j][i] * inverse for i in below}
            factor[b] = jnp.where(row_id > j, factor[b], 0.0)
            for k in range(j + 1, GROUP):
                row = spread_row(col[k][b], j)
                for i in below:
                    col[k][i] = col[k][i] - factor[i] * row
            for h in range(halves):
                row = spread_row(x[b][h], j)
                for i in below:
                    x[i][h] = x[i][h] - factor[i] * row
            if b + 1 < groups:
                row = spread_row(g[b], j)
                for i in below:
                    g[i] = g[i] - factor[i] * row
        scale = lax.rsqrt(pivots)
        for h in range(halves):
            x[b][h] = x[b][h] * scale
        if (b + 1) * GROUP % HALF == 0:
            done = x[b + 1 - HALF // GROUP : b + 1]
            yield jnp.concatenate([jnp.concatenate(parts, axis=1) for parts in done], axis=0)


def kernel(
    n, experts, count,
    grad, error, q_init,
    basis, q_out, new_error, norm,
    g_buf, e_buf, comb, theirs, pair, fac0, fac,
    s2_send, s2_recv, own, p, n1, n2,
    g_sem, e_sem, q_sem, o_sem,
    s1_ss, s1_rs, s2_ss, s2_rs, p_ss, p_rs,
    ag_ss, fw_ss, ag_rs, n1_ss, n1_rs, n2_ss, n2_rs,
):
    me = lax.axis_index("dp")
    place = lax.axis_index("expert")
    chip, core = lax.div(me, 2), lax.rem(me, 2)
    partner = 2 * chip + 1 - core
    chips = n // 2
    rows, share, rank = comb.shape[1], comb.shape[2], fac0.shape[1]

    def send(src, dst, ssem, rsem, **where):
        return pltpu.make_async_remote_copy(
            src_ref=src, dst_ref=dst, send_sem=ssem, recv_sem=rsem, device_id=where, device_id_type=MESH
        )

    def columns(ref, j):
        return ref.at[:, pl.ds(pl.multiple_of(j * share, share), share)]

    def load(j):
        return (
            pltpu.make_async_copy(columns(grad, j), g_buf.at[j], g_sem.at[j]),
            pltpu.make_async_copy(columns(error, j), e_buf.at[j], e_sem.at[j]),
            pltpu.make_async_copy(columns(q_init, j), fac0.at[j], q_sem.at[j]),
        )

    def combine(j, total):
        for copy in load(j):
            copy.wait()
        comb[j] = (g_buf[j].astype(F32) + e_buf[j].astype(F32)).astype(BF16)
        return total + lax.dot_general(comb[j], fac0[j], NT, preferred_element_type=F32)

    def hand_over(t):
        return send(comb.at[2 * t + 1 - core], theirs.at[t], s1_ss.at[t], s1_rs.at[t], dp=partner)

    for t in range(chips):
        for copy in load(2 * t + 1 - core):
            copy.start()
    for t in range(chips):
        for copy in load(2 * t + core):
            copy.start()

    barrier = pltpu.get_barrier_semaphore()
    for s in range(1, n):
        pl.semaphore_signal(barrier, inc=1, device_id={"dp": lax.rem(me + s, n)}, device_id_type=MESH)
    for s in range(1, experts):
        pl.semaphore_signal(
            barrier, inc=1, device_id={"expert": lax.rem(place + s, experts)}, device_id_type=MESH
        )

    total = combine(1 - core, jnp.zeros((rows, rank), F32))
    pl.semaphore_wait(barrier, n - 1 + experts - 1)
    hand_over(0).start()

    def first(t, total):
        total = combine(2 * t + 1 - core, total)
        hand_over(t).start()
        return total

    total = lax.fori_loop(1, chips, first, total)
    total = lax.fori_loop(0, chips, lambda t, total: combine(2 * t + core, total), total)

    def add_pair(t, _):
        hand_over(t).wait_recv()
        pair[t] = (comb[2 * t + core].astype(F32) + theirs[t].astype(F32)).astype(BF16)
        return 0

    pending = []
    for it in range(ITERS):
        last = it == ITERS - 1
        p[it, me] = jnp.transpose(total).astype(BF16)
        copies = []
        for s in range(n - 1, 0, -1):
            copies.append(
                send(p.at[it, me], p.at[it, me], p_ss.at[it, s], p_rs.at[it, s], dp=xor(me, s, n))
            )
            copies[-1].start()
        if it == 0:
            lax.fori_loop(0, chips, add_pair, 0)
        for copy in copies:
            copy.wait_recv()
        pending += copies
        pt = p[it, 0].astype(F32)
        for j in range(1, n):
            pt = pt + p[it, j].astype(F32)
        pt = pt / n
        second_hop, ortho = [], []
        for h, part in enumerate(orthonormal_rows(pt)):
            ortho.append(part)
            low = part.astype(BF16)
            second_hop.append([])
            for s in range(chips - 1, -1, -1):
                q = jnp.dot(low, pair[xor(chip, s, chips)], preferred_element_type=F32)
                if s:
                    s2_send[it, h, s] = q.astype(BF16)
                    copy = send(
                        s2_send.at[it, h, s], s2_recv.at[it, h, s], s2_ss.at[it, h, s], s2_rs.at[it, h, s],
                        dp=2 * xor(chip, s, chips) + core,
                    )
                    copy.start()
                    second_hop[h].append(copy)
                else:
                    own[h] = q

        def half(j, h, it=it):
            return fac.at[it, j, pl.ds(h * HALF, HALF), :]

        halves = rank // HALF
        for h in range(halves):
            for copy in second_hop[h]:
                copy.wait_recv()
            q = own[h]
            for s in range(1, chips):
                q = q + s2_recv[it, h, s].astype(F32)
            q = q / n
            if last:
                q_out[h * HALF : (h + 1) * HALF, :] = q
            fac[it, me, h * HALF : (h + 1) * HALF, :] = q.astype(BF16)
            for s in range(chips - 1, -1 if last else 0, -1):
                target = partner if s == 0 else 2 * xor(chip, s, chips) + core
                copy = send(half(me, h), half(me, h), ag_ss.at[it, h, s], ag_rs.at[it, h, me], dp=target)
                copy.start()
                pending.append(copy)
            pending += second_hop[h]
        if last:
            ortho = jnp.concatenate(ortho, axis=0)
            basis[...] = ortho
            low_t = jnp.transpose(ortho).astype(BF16)

        def forward(s, j, h, half=half, it=it):
            return send(half(j, h), half(j, h), fw_ss.at[h, s], ag_rs.at[it, h, j], dp=partner)

        def arrived(j, onward=None):
            for h in range(halves):
                forward(0, j, h).wait_recv()
                if onward is not None:
                    forward(onward, j, h).start()

        if not last:
            def use(t, value, it=it):
                return value + lax.dot_general(pair[t], fac[it, 2 * t + core], NT, preferred_element_type=F32)

            def step(s, value):
                t = xor(chip, s, chips)
                arrived(2 * t + core)
                return use(t, value)

            value = use(chip, jnp.zeros((rows, rank), F32))
        else:
            def use(j, value, it=it):
                approx = jnp.dot(low_t, fac[it, j], preferred_element_type=F32)
                residual = (comb[j].astype(F32) - approx).astype(BF16)
                g_buf[j] = residual
                pltpu.make_async_copy(g_buf.at[j], columns(new_error, j), o_sem.at[j]).start()
                wide = residual.astype(F32)
                squares = jnp.sum((wide * wide).reshape(rows // GROUP, GROUP, share), axis=0)
                for h in range(share // LANES):
                    value = value + squares[:, LANES * h : LANES * (h + 1)]
                return value

            def step(s, value):
                t = xor(chip, s, chips)
                arrived(2 * t + core, s)
                value = use(2 * t + core, value)
                arrived(2 * t + 1 - core)
                return use(2 * t + 1 - core, value)

            value = use(me, jnp.zeros(n1.shape[1:], F32))
            arrived(partner)
            value = use(partner, value)

        total = lax.fori_loop(1, chips, step, value)

    n1[me] = total
    copies = [
        send(n1.at[me], n1.at[me], n1_ss.at[s], n1_rs.at[s], dp=lax.rem(me + s, n)) for s in range(1, n)
    ]
    for copy in copies:
        copy.start()
    for copy in copies:
        copy.wait_recv()
    pending += copies
    total = n1[0]
    for j in range(1, n):
        total = total + n1[j]
    n2[place] = total
    copies = [
        send(n2.at[place], n2.at[place], n2_ss.at[s], n2_rs.at[s], expert=lax.rem(place + s, experts))
        for s in range(1, experts)
    ]
    for copy in copies:
        copy.start()
    for copy in copies:
        copy.wait_recv()
    pending += copies
    total = n2[0]
    for j in range(1, experts):
        total = total + n2[j]
    norm[...] = jnp.sqrt(jnp.sum(total, keepdims=True) / count)

    for copy in pending:
        copy.wait_send()
    for s in range(1, chips):
        for h in range(halves):
            forward(s, 2 * xor(chip, s, chips) + core, h).wait_send()
    for t in range(chips):
        hand_over(t).wait_send()
    for j in range(n):
        pltpu.make_async_copy(g_buf.at[j], columns(new_error, j), o_sem.at[j]).wait()


def hand_out_kernel(basis, q, new_error, basis_out, q_out, new_error_out, sem):
    parts = sem.shape[0] - 2
    height = new_error.shape[0] // parts

    def piece(ref, i):
        return ref.at[pl.ds(i * height, height), :]

    moves = [(piece(new_error, i), piece(new_error_out, i)) for i in range(parts)]
    moves += [(basis, basis_out), (q, q_out)]
    copies = [pltpu.make_async_copy(a, b, sem.at[i]) for i, (a, b) in enumerate(moves)]
    for copy in copies:
        copy.start()
    for copy in copies:
        copy.wait()


def hand_out(*arrays):
    hbm = pl.BlockSpec(memory_space=pl.ANY)
    return pl.pallas_call(
        hand_out_kernel,
        out_shape=tuple(jax.ShapeDtypeStruct(a.shape, a.dtype) for a in arrays),
        in_specs=[hbm] * 3,
        out_specs=(hbm,) * 3,
        scratch_shapes=[pltpu.SemaphoreType.DMA((16 + 2,))],
        compiler_params=pltpu.CompilerParams(vmem_limit_bytes=32 * 2**20),
    )(*arrays)


def local(grad, error, q_init):
    n, experts = lax.axis_size("dp"), lax.axis_size("expert")
    rows, width = grad.shape[2:]
    rank = q_init.shape[1]
    share = width // n
    chips = n // 2
    count = rows * width * n * experts
    dma = pltpu.SemaphoreType.DMA
    vmem, hbm = pl.BlockSpec(memory_space=pltpu.VMEM), pl.BlockSpec(memory_space=pl.ANY)
    halves = rank // HALF
    hop = pltpu.VMEM((ITERS, halves, chips, HALF, share), BF16)
    basis, q, new_error, norm = pl.pallas_call(
        functools.partial(kernel, n, experts, count),
        out_shape=(
            jax.ShapeDtypeStruct((rank, rows), F32),
            jax.ShapeDtypeStruct((rank, share), F32),
            jax.ShapeDtypeStruct((rows, width), BF16),
            jax.ShapeDtypeStruct((1, 1), F32),
        ),
        in_specs=[hbm, hbm, hbm],
        out_specs=(vmem, vmem, hbm, vmem),
        scratch_shapes=[
            pltpu.VMEM((n, rows, share), BF16),
            pltpu.VMEM((n, rows, share), BF16),
            pltpu.VMEM((n, rows, share), BF16),
            pltpu.VMEM((chips, rows, share), BF16),
            pltpu.VMEM((chips, rows, share), BF16),
            pltpu.VMEM((n, rank, share), BF16),
            pltpu.VMEM((ITERS, n, rank, share), BF16),
            hop, hop,
            pltpu.VMEM((halves, HALF, share), F32),
            pltpu.VMEM((ITERS, n, rank, rows), BF16),
            pltpu.VMEM((n, GROUP, LANES), F32),
            pltpu.VMEM((experts, GROUP, LANES), F32),
            dma((n,)), dma((n,)), dma((n,)), dma((n,)),
            dma((chips,)), dma((chips,)), dma((ITERS, halves, chips)), dma((ITERS, halves, chips)),
            dma((ITERS, n)), dma((ITERS, n)),
            dma((ITERS, halves, chips)), dma((halves, chips)), dma((ITERS, halves, n)),
            dma((n,)), dma((n,)), dma((experts,)), dma((experts,)),
        ],
        compiler_params=pltpu.CompilerParams(
            collective_id=0, has_side_effects=True, vmem_limit_bytes=49 * 2**20
        ),
        cost_estimate=pl.CostEstimate(
            flops=2 * 5 * rows * rank * width, bytes_accessed=6 * rows * width, transcendentals=0
        ),
    )(grad[0, 0], error[0, 0], q_init[0])
    basis, q, new_error = hand_out(basis, q, new_error)
    return (jnp.transpose(basis)[None], q[None], new_error[None, None], norm[0, 0])


def solution(mesh):
    placed = (P("expert", "dp", None, None), P("expert", "dp", None, None), P("expert", None, None))
    return jax.shard_map(
        local,
        mesh=mesh,
        in_specs=placed,
        out_specs=(
            P("expert", None, None),
            P("expert", None, "dp"),
            P("expert", "dp", None, None),
            P(),
        ),
        check_vma=False,
    )
```

```python
import functools

import jax
import jax.numpy as jnp
from jax import lax
from jax.experimental import pallas as pl
from jax.experimental.pallas import tpu as pltpu
from jax.sharding import PartitionSpec as P

ITERS = 2
MESH = pl.DeviceIdType.MESH
F32 = jnp.float32
BF16 = jnp.bfloat16
LANES = 128
GROUP = 8
HALF = 16
NT = (((1,), (1,)), ((), ()))


def xor(a, b, size):
    out, bit = 0, 1
    while bit < size:
        out = out + bit * lax.rem(lax.div(a, bit) + lax.div(b, bit), 2)
        bit *= 2
    return out


def spread_row(tile, j):
    return jnp.broadcast_to(tile[j : j + 1, :], tile.shape)


def inverted(x):
    guess = pl.reciprocal(x, approx=True)
    for _ in range(2):
        guess = guess * (2.0 - x * guess)
    return guess


def orthonormal_rows(pt):
    rank, rows = pt.shape
    groups, halves = rank // GROUP, rows // LANES
    padded = jnp.concatenate([pt, jnp.zeros((LANES - rank, rows), F32)], axis=0)
    gram = lax.dot_general(pt, padded, NT, precision=lax.Precision.HIGHEST, preferred_element_type=F32)
    g = [gram[GROUP * i : GROUP * (i + 1), :] for i in range(groups)]
    x = [
        [pt[GROUP * i : GROUP * (i + 1), LANES * h : LANES * (h + 1)] for h in range(halves)]
        for i in range(groups)
    ]
    row_id = lax.broadcasted_iota(jnp.int32, (GROUP, LANES), 0)
    for b in range(groups):
        below = range(b, groups)
        col = [
            {i: jnp.broadcast_to(g[i][:, GROUP * b + j : GROUP * b + j + 1], (GROUP, LANES)) for i in below}
            for j in range(GROUP)
        ]
        pivots = jnp.ones((GROUP, LANES), F32)
        for j in range(GROUP):
            pivot = spread_row(col[j][b], j)
            pivots = jnp.where(row_id == j, pivot, pivots)
            inverse = inverted(pivot)
            col[j][b] = jnp.where(row_id > j, col[j][b], 0.0)
            factor = {i: col[j][i] * inverse for i in below}
            for k in range(j + 1, GROUP):
                row = spread_row(col[k][b], j)
                for i in below:
                    col[k][i] = col[k][i] - factor[i] * row
            for h in range(halves):
                row = spread_row(x[b][h], j)
                for i in below:
                    x[i][h] = x[i][h] - factor[i] * row
            if b + 1 < groups:
                row = spread_row(g[b], j)
                for i in below:
                    g[i] = g[i] - factor[i] * row
        scale = lax.rsqrt(pivots)
        for h in range(halves):
            x[b][h] = x[b][h] * scale
        if (b + 1) * GROUP % HALF == 0:
            done = x[b + 1 - HALF // GROUP : b + 1]
            yield jnp.concatenate([jnp.concatenate(parts, axis=1) for parts in done], axis=0)


def kernel(
    n, experts, count,
    grad, error, q_init,
    basis, q_out, new_error, norm,
    g_buf, e_buf, comb, theirs, pair, fac0, fac,
    s2_send, s2_recv, own, p, n1, n2,
    g_sem, e_sem, q_sem, o_sem,
    s1_ss, s1_rs, s2_ss, s2_rs, p_ss, p_rs,
    ag_ss, fw_ss, ag_rs, n1_ss, n1_rs, n2_ss, n2_rs,
):
    me = lax.axis_index("dp")
    place = lax.axis_index("expert")
    chip, core = lax.div(me, 2), lax.rem(me, 2)
    partner = 2 * chip + 1 - core
    chips = n // 2
    rows, share, rank = comb.shape[1], comb.shape[2], fac0.shape[1]

    def send(src, dst, ssem, rsem, **where):
        return pltpu.make_async_remote_copy(
            src_ref=src, dst_ref=dst, send_sem=ssem, recv_sem=rsem, device_id=where, device_id_type=MESH
        )

    def columns(ref, j):
        return ref.at[:, pl.ds(pl.multiple_of(j * share, share), share)]

    def load(j):
        return (
            pltpu.make_async_copy(columns(grad, j), g_buf.at[j], g_sem.at[j]),
            pltpu.make_async_copy(columns(error, j), e_buf.at[j], e_sem.at[j]),
            pltpu.make_async_copy(columns(q_init, j), fac0.at[j], q_sem.at[j]),
        )

    def combine(j, total):
        for copy in load(j):
            copy.wait()
        comb[j] = (g_buf[j].astype(F32) + e_buf[j].astype(F32)).astype(BF16)
        return total + lax.dot_general(comb[j], fac0[j], NT, preferred_element_type=F32)

    def hand_over(t):
        return send(comb.at[2 * t + 1 - core], theirs.at[t], s1_ss.at[t], s1_rs.at[t], dp=partner)

    for t in range(chips):
        for copy in load(2 * t + 1 - core):
            copy.start()
    for t in range(chips):
        for copy in load(2 * t + core):
            copy.start()

    barrier = pltpu.get_barrier_semaphore()
    for s in range(1, n):
        pl.semaphore_signal(barrier, inc=1, device_id={"dp": lax.rem(me + s, n)}, device_id_type=MESH)
    for s in range(1, experts):
        pl.semaphore_signal(
            barrier, inc=1, device_id={"expert": lax.rem(place + s, experts)}, device_id_type=MESH
        )

    total = combine(1 - core, jnp.zeros((rows, rank), F32))
    pl.semaphore_wait(barrier, n - 1 + experts - 1)
    hand_over(0).start()

    def first(t, total):
        total = combine(2 * t + 1 - core, total)
        hand_over(t).start()
        return total

    total = lax.fori_loop(1, chips, first, total)
    total = lax.fori_loop(0, chips, lambda t, total: combine(2 * t + core, total), total)

    def add_pair(t, _):
        hand_over(t).wait_recv()
        pair[t] = (comb[2 * t + core].astype(F32) + theirs[t].astype(F32)).astype(BF16)
        return 0

    pending = []
    for it in range(ITERS):
        last = it == ITERS - 1
        p[it, me] = jnp.transpose(total).astype(BF16)
        copies = []
        for s in range(n - 1, 0, -1):
            copies.append(
                send(p.at[it, me], p.at[it, me], p_ss.at[it, s], p_rs.at[it, s], dp=xor(me, s, n))
            )
            copies[-1].start()
        if it == 0:
            lax.fori_loop(0, chips, add_pair, 0)
        for copy in copies:
            copy.wait_recv()
        pending += copies
        pt = p[it, 0].astype(F32)
        for j in range(1, n):
            pt = pt + p[it, j].astype(F32)
        pt = pt / n
        second_hop, ortho = [], []
        for h, part in enumerate(orthonormal_rows(pt)):
            ortho.append(part)
            low = part.astype(BF16)
            second_hop.append([])
            for s in range(chips - 1, -1, -1):
                q = jnp.dot(low, pair[xor(chip, s, chips)], preferred_element_type=F32)
                if s:
                    s2_send[it, h, s] = q.astype(BF16)
                    copy = send(
                        s2_send.at[it, h, s], s2_recv.at[it, h, s], s2_ss.at[it, h, s], s2_rs.at[it, h, s],
                        dp=2 * xor(chip, s, chips) + core,
                    )
                    copy.start()
                    second_hop[h].append(copy)
                else:
                    own[h] = q

        def half(j, h, it=it):
            return fac.at[it, j, pl.ds(h * HALF, HALF), :]

        halves = rank // HALF
        for h in range(halves):
            for copy in second_hop[h]:
                copy.wait_recv()
            q = own[h]
            for s in range(1, chips):
                q = q + s2_recv[it, h, s].astype(F32)
            q = q / n
            if last:
                q_out[h * HALF : (h + 1) * HALF, :] = q
            fac[it, me, h * HALF : (h + 1) * HALF, :] = q.astype(BF16)
            for s in range(chips - 1, -1 if last else 0, -1):
                target = partner if s == 0 else 2 * xor(chip, s, chips) + core
                copy = send(half(me, h), half(me, h), ag_ss.at[it, h, s], ag_rs.at[it, h, me], dp=target)
                copy.start()
                pending.append(copy)
            pending += second_hop[h]
        if last:
            ortho = jnp.concatenate(ortho, axis=0)
            basis[...] = ortho
            low_t = jnp.transpose(ortho).astype(BF16)

        def forward(s, j, h, half=half, it=it):
            return send(half(j, h), half(j, h), fw_ss.at[h, s], ag_rs.at[it, h, j], dp=partner)

        def arrived(j, onward=None):
            for h in range(halves):
                forward(0, j, h).wait_recv()
                if onward is not None:
                    forward(onward, j, h).start()

        if not last:
            def use(t, value, it=it):
                return value + lax.dot_general(pair[t], fac[it, 2 * t + core], NT, preferred_element_type=F32)

            def step(s, value):
                t = xor(chip, s, chips)
                arrived(2 * t + core)
                return use(t, value)

            value = use(chip, jnp.zeros((rows, rank), F32))
        else:
            def use(j, value, it=it):
                approx = jnp.dot(low_t, fac[it, j], preferred_element_type=F32)
                residual = (comb[j].astype(F32) - approx).astype(BF16)
                g_buf[j] = residual
                pltpu.make_async_copy(g_buf.at[j], columns(new_error, j), o_sem.at[j]).start()
                wide = residual.astype(F32)
                squares = jnp.sum((wide * wide).reshape(rows // GROUP, GROUP, share), axis=0)
                for h in range(share // LANES):
                    value = value + squares[:, LANES * h : LANES * (h + 1)]
                return value

            def step(s, value):
                t = xor(chip, s, chips)
                arrived(2 * t + core, s)
                value = use(2 * t + core, value)
                arrived(2 * t + 1 - core)
                return use(2 * t + 1 - core, value)

            value = use(me, jnp.zeros(n1.shape[1:], F32))
            arrived(partner)
            value = use(partner, value)

        total = lax.fori_loop(1, chips, step, value)

    n1[me] = total
    copies = [
        send(n1.at[me], n1.at[me], n1_ss.at[s], n1_rs.at[s], dp=lax.rem(me + s, n)) for s in range(1, n)
    ]
    for copy in copies:
        copy.start()
    for copy in copies:
        copy.wait_recv()
    pending += copies
    total = n1[0]
    for j in range(1, n):
        total = total + n1[j]
    n2[place] = total
    copies = [
        send(n2.at[place], n2.at[place], n2_ss.at[s], n2_rs.at[s], expert=lax.rem(place + s, experts))
        for s in range(1, experts)
    ]
    for copy in copies:
        copy.start()
    for copy in copies:
        copy.wait_recv()
    pending += copies
    total = n2[0]
    for j in range(1, experts):
        total = total + n2[j]
    norm[...] = jnp.sqrt(jnp.sum(total, keepdims=True) / count)

    for copy in pending:
        copy.wait_send()
    for s in range(1, chips):
        for h in range(halves):
            forward(s, 2 * xor(chip, s, chips) + core, h).wait_send()
    for t in range(chips):
        hand_over(t).wait_send()
    for j in range(n):
        pltpu.make_async_copy(g_buf.at[j], columns(new_error, j), o_sem.at[j]).wait()


def hand_out_kernel(basis, q, new_error, basis_out, q_out, new_error_out, sem):
    parts = sem.shape[0] - 2
    height = new_error.shape[0] // parts

    def piece(ref, i):
        return ref.at[pl.ds(i * height, height), :]

    moves = [(piece(new_error, i), piece(new_error_out, i)) for i in range(parts)]
    moves += [(basis, basis_out), (q, q_out)]
    copies = [pltpu.make_async_copy(a, b, sem.at[i]) for i, (a, b) in enumerate(moves)]
    for copy in copies:
        copy.start()
    for copy in copies:
        copy.wait()


def hand_out(*arrays):
    hbm = pl.BlockSpec(memory_space=pl.ANY)
    return pl.pallas_call(
        hand_out_kernel,
        out_shape=tuple(jax.ShapeDtypeStruct(a.shape, a.dtype) for a in arrays),
        in_specs=[hbm] * 3,
        out_specs=(hbm,) * 3,
        scratch_shapes=[pltpu.SemaphoreType.DMA((16 + 2,))],
        compiler_params=pltpu.CompilerParams(vmem_limit_bytes=32 * 2**20),
    )(*arrays)


def local(grad, error, q_init):
    n, experts = lax.axis_size("dp"), lax.axis_size("expert")
    rows, width = grad.shape[2:]
    rank = q_init.shape[1]
    share = width // n
    chips = n // 2
    count = rows * width * n * experts
    dma = pltpu.SemaphoreType.DMA
    vmem, hbm = pl.BlockSpec(memory_space=pltpu.VMEM), pl.BlockSpec(memory_space=pl.ANY)
    halves = rank // HALF
    hop = pltpu.VMEM((ITERS, halves, chips, HALF, share), BF16)
    basis, q, new_error, norm = pl.pallas_call(
        functools.partial(kernel, n, experts, count),
        out_shape=(
            jax.ShapeDtypeStruct((rank, rows), F32),
            jax.ShapeDtypeStruct((rank, share), F32),
            jax.ShapeDtypeStruct((rows, width), BF16),
            jax.ShapeDtypeStruct((1, 1), F32),
        ),
        in_specs=[hbm, hbm, hbm],
        out_specs=(vmem, vmem, hbm, vmem),
        scratch_shapes=[
            pltpu.VMEM((n, rows, share), BF16),
            pltpu.VMEM((n, rows, share), BF16),
            pltpu.VMEM((n, rows, share), BF16),
            pltpu.VMEM((chips, rows, share), BF16),
            pltpu.VMEM((chips, rows, share), BF16),
            pltpu.VMEM((n, rank, share), BF16),
            pltpu.VMEM((ITERS, n, rank, share), BF16),
            hop, hop,
            pltpu.VMEM((halves, HALF, share), F32),
            pltpu.VMEM((ITERS, n, rank, rows), BF16),
            pltpu.VMEM((n, GROUP, LANES), F32),
            pltpu.VMEM((experts, GROUP, LANES), F32),
            dma((n,)), dma((n,)), dma((n,)), dma((n,)),
            dma((chips,)), dma((chips,)), dma((ITERS, halves, chips)), dma((ITERS, halves, chips)),
            dma((ITERS, n)), dma((ITERS, n)),
            dma((ITERS, halves, chips)), dma((halves, chips)), dma((ITERS, halves, n)),
            dma((n,)), dma((n,)), dma((experts,)), dma((experts,)),
        ],
        compiler_params=pltpu.CompilerParams(
            collective_id=0, has_side_effects=True, vmem_limit_bytes=49 * 2**20
        ),
        cost_estimate=pl.CostEstimate(
            flops=2 * 5 * rows * rank * width, bytes_accessed=6 * rows * width, transcendentals=0
        ),
    )(grad[0, 0], error[0, 0], q_init[0])
    basis, q, new_error = hand_out(basis, q, new_error)
    return (jnp.transpose(basis)[None], q[None], new_error[None, None], norm[0, 0])


def solution(mesh):
    placed = (P("expert", "dp", None, None), P("expert", "dp", None, None), P("expert", None, None))
    return jax.shard_map(
        local,
        mesh=mesh,
        in_specs=placed,
        out_specs=(
            P("expert", None, None),
            P("expert", None, "dp"),
            P("expert", "dp", None, None),
            P(),
        ),
        check_vma=False,
    )
```
